32 devices in a mesh: dp: 4 (over x, core), depth: 2 (over y), height: 4 (over z).
Axes of the slice: x: 2, y: 2, z: 4, core: 2. Of those that a mesh axis runs over, the one named last changes fastest.
Arguments:
- act_one: bfloat16 [4, 32, 8, 64, 128], P('dp', None, 'depth', 'height'), may hold values from -6 to 6
- pre_two: bfloat16 [4, 64, 8, 64, 128], P('dp', None, 'depth', 'height'), may hold values from -6 to 6
- cot_three: bfloat16 [4, 128, 4, 2048], P('dp', None, 'depth', 'height'), may hold values from -24 to 24
- weight_two: float32 [64, 864], replicated, may hold values from -6 to 6
- weight_three: float32 [128, 1728], replicated, may hold values from -6 to 6
- moment_two: float32 [55296], P(('dp', 'depth', 'height')), may hold values from -1.2 to 1.2
- moment_three: float32 [221184], P(('dp', 'depth', 'height')), may hold values from -1.2 to 1.2
Outputs:
- grad_input: bfloat16 [4, 32, 8, 64, 128], P('dp', None, 'depth', 'height')
- new_weight_two: float32 [64, 864], replicated
- new_weight_three: float32 [128, 1728], replicated
- new_moment_two: float32 [55296], P(('dp', 'depth', 'height'))
- new_moment_three: float32 [221184], P(('dp', 'depth', 'height'))
The draws below stay inside these ranges and needn't reach their ends.
All inputs are finite; a program needn't handle non-finite values.
Results may differ from the reference program's by a relative error of at most 0.007.
Values may be sent and summed in bfloat16 or wider, within the bound.
A program may use at most 128 MiB of HBM per device.

```python
import jax
import jax.numpy as jnp
from jax import lax

C1 = 32
C2 = 64
C3 = 128
CW = 128
VOLUMES = 4
D1 = 8
H1 = 64
P2 = 55296
P3 = 221184
N_DP = 4


def levels(rng, shape, shards, low, largest):
    def one(axis_at, parts):
        steps = jax.random.uniform(jax.random.fold_in(jax.random.fold_in(rng, 6), axis_at), (parts,), jnp.float32, low / len(shards), largest / len(shards))
        return jnp.repeat(jnp.exp(steps), shape[axis_at] // parts).reshape((-1,) + (1,) * (len(shape) - axis_at - 1))

    level = one(*shards[0])
    for cut in shards[1:]:
        level = level * one(*cut)
    return level


def bell_draw(key, dims, deviation, reach, pieces=(), held_as=jnp.bfloat16):
    values = deviation * jax.random.normal(key, dims, jnp.float32)
    if pieces:
        values = values * levels(key, dims, pieces, -0.22, 0.18)
    return jnp.clip(values, -reach, reach).astype(held_as)


def setup_inputs(seed: int = 0) -> dict:
    arg_keys = jax.random.split(jax.random.key(seed), 8)
    act_one = bell_draw(arg_keys[0], (VOLUMES, C1, D1, H1, CW), 1.0, 6.0, ((0, 4), (2, 2), (3, 4)))
    pre_two = bell_draw(arg_keys[1], (VOLUMES, C2, D1, H1, CW), 1.0, 6.0, ((0, 4), (2, 2), (3, 4)))
    cot_three = bell_draw(arg_keys[2], (VOLUMES, C3, D1 // 2, (H1 // 2) * (CW // 2)), 4.0, 24.0, ((0, 4), (2, 2), (3, 4)))
    weight_two = bell_draw(arg_keys[3], (C2, C1 * 27), 1.0, 6.0, (), jnp.float32)
    weight_three = bell_draw(arg_keys[4], (C3, C2 * 27), 1.0, 6.0, (), jnp.float32)
    moment_two = bell_draw(arg_keys[5], (P2,), 0.2, 1.2, ((0, 32),), jnp.float32)
    moment_three = bell_draw(arg_keys[6], (P3,), 0.2, 1.2, ((0, 32),), jnp.float32)
    return dict(act_one=act_one, pre_two=pre_two, cot_three=cot_three, weight_two=weight_two, weight_three=weight_three, moment_two=moment_two, moment_three=moment_three)


SLOPE = 0.3
LEARN = 4.0
TRUST = 0.05
MOMENTUM = 0.9
EPSILON = 1e-06

def leaky(value):
    return jnp.where(value > 0, value, SLOPE * value)

def slope_of(value):
    return jnp.where(value > 0, 1.0, SLOPE).astype(jnp.float32)

def lars(weight, grad, moment):
    flat_grad = grad.reshape(-1)
    trust = TRUST * jnp.sqrt(jnp.sum(weight * weight)) / (jnp.sqrt(jnp.sum(flat_grad * flat_grad)) + EPSILON)
    new_moment = MOMENTUM * moment + LEARN * trust * flat_grad
    return (weight - new_moment.reshape(weight.shape), new_moment)

def reference(act_one, pre_two, cot_three, weight_two, weight_three, moment_two, moment_three):
    deep = D1 // 2
    tall = H1 // 2
    broad = CW // 2
    scale_two = (C1 * 27) ** (-0.5)
    scale_three = (C2 * 27) ** (-0.5)
    wb_two = weight_two.astype(jnp.bfloat16).astype(jnp.float32).reshape(C2, C1, 27)
    wb_three = weight_three.astype(jnp.bfloat16).astype(jnp.float32).reshape(C3, C2, 27)

    def one_volume(inputs):
        act, pre, cot = inputs
        pre_f = pre.astype(jnp.float32)
        pooled = leaky(pre_f).reshape(C2, deep, 2, tall, 2, broad, 2).mean(axis=(2, 4, 6)).astype(jnp.bfloat16)
        pooled_f = pooled.astype(jnp.float32)
        cot_f = cot.reshape(C3, deep, tall, broad).astype(jnp.float32)
        cot_pad = jnp.pad(cot_f, ((0, 0), (1, 1), (1, 1), (1, 1)))
        back = jnp.zeros((C2, deep, tall, broad), jnp.float32)
        grads_three = []
        for k in range(27):
            kd, kh, kw = (k // 9, k // 3 % 3, k % 3)
            od, oh, ow = (2 - kd, 2 - kh, 2 - kw)
            piece = cot_pad[:, od:od + deep, oh:oh + tall, ow:ow + broad]
            back = back + jnp.einsum('oi,odhw->idhw', wb_three[:, :, k], piece)
            grads_three.append(jnp.einsum('odhw,idhw->oi', piece, pooled_f))
        back = (scale_three * back).astype(jnp.bfloat16).astype(jnp.float32)
        upper = jnp.broadcast_to(back.reshape(C2, deep, 1, tall, 1, broad, 1), (C2, deep, 2, tall, 2, broad, 2))
        upper = upper.reshape(C2, D1, H1, CW)
        cot_two = (upper * 0.125 * slope_of(pre_f)).astype(jnp.bfloat16).astype(jnp.float32)
        two_pad = jnp.pad(cot_two, ((0, 0), (1, 1), (1, 1), (1, 1)))
        act_f = act.astype(jnp.float32)
        into = jnp.zeros((C1, D1, H1, CW), jnp.float32)
        grads_two = []
        for k in range(27):
            kd, kh, kw = (k // 9, k // 3 % 3, k % 3)
            od, oh, ow = (2 - kd, 2 - kh, 2 - kw)
            piece = two_pad[:, od:od + D1, oh:oh + H1, ow:ow + CW]
            into = into + jnp.einsum('oi,odhw->idhw', wb_two[:, :, k], piece)
            grads_two.append(jnp.einsum('odhw,idhw->oi', piece, act_f))
        grad_in = (scale_two * into).astype(jnp.bfloat16)
        return (grad_in, jnp.stack(grads_two, -1).reshape(C2, C1 * 27), jnp.stack(grads_three, -1).reshape(C3, C2 * 27))
    grad_input, part_two, part_three = lax.map(one_volume, (act_one, pre_two, cot_three))
    grad_two = lax.optimization_barrier(jnp.sum(part_two, axis=0)) * (scale_two / N_DP)
    grad_three = lax.optimization_barrier(jnp.sum(part_three, axis=0)) * (scale_three / N_DP)
    new_weight_two, new_moment_two = lars(weight_two, grad_two, moment_two)
    new_weight_three, new_moment_three = lars(weight_three, grad_three, moment_three)
    return (grad_input, new_weight_two, new_weight_three, new_moment_two, new_moment_three)
```

```python
import functools

import jax
import jax.numpy as jnp
from jax import lax
from jax.experimental import pallas as pl
from jax.experimental.pallas import tpu as pltpu
from jax.sharding import PartitionSpec as P

AXES = ("dp", "depth", "height")
MESH = pl.DeviceIdType.MESH

SLOPE = 0.3
LEARN = 4.0
TRUST = 0.05
MOMENTUM = 0.9
EPSILON = 1e-06


def padded_2(x, sides, width):
    for axis, dim in sides:
        devices, length = (lax.axis_size(axis), x.shape[dim])
        up = [(i, (i + 1) % devices) for i in range(devices - 1)]
        down = [(j, i) for i, j in up]
        last = lax.slice_in_dim(x, length - width, length, axis=dim)
        initial = lax.slice_in_dim(x, 0, width, axis=dim)
        before = lax.ppermute(last, axis, up)
        after = lax.ppermute(initial, axis, down)
        x = jnp.concatenate([before, x, after], axis=dim)
    return x


def leaky(value):
    return jnp.where(value > 0, value, SLOPE * value)


def slope_of(value):
    return jnp.where(value > 0, 1.0, SLOPE).astype(jnp.float32)


def partners(sizes, me):
    out = []
    for axis, size in enumerate(sizes):
        group = []
        for step in range(1, size):
            other = lax.rem(me[axis] + step, size)
            group.append((other, tuple(other if i == axis else me[i] for i in range(3))))
        out.append(group)
    return out


def update_kernel(
    sizes, rows_two, scales, g_ref, m_ref, norm_ref, mom_ref, all_ref,
    recv_a, recv_b, recv_c, send_b, send_c, sum_send, sum_recv, send_sem, recv_sem,
):
    me = [lax.axis_index(name) for name in AXES]
    groups = partners(sizes, me)
    count = sum(size - 1 for size in sizes)
    barrier = pltpu.get_barrier_semaphore()
    for group in groups:
        for _, device in group:
            pl.semaphore_signal(barrier, inc=1, device_id=device, device_id_type=MESH)
    pl.semaphore_wait(barrier, count)

    def exchange(axis, phase, source, target):
        base = phase * count + sum(size - 1 for size in sizes[:axis])
        copies = []
        for j, (other, device) in enumerate(groups[axis]):
            copy = pltpu.make_async_remote_copy(
                src_ref=source(other),
                dst_ref=target(j),
                send_sem=send_sem.at[base + j],
                recv_sem=recv_sem.at[base + j],
                device_id=device,
                device_id_type=MESH,
            )
            copy.start()
            copies.append(copy)
        for copy in copies:
            copy.wait()

    exchange(0, 0, lambda other: g_ref.at[other], lambda j: recv_a.at[j])
    total = g_ref[me[0]].astype(jnp.float32)
    for j in range(sizes[0] - 1):
        total = total + recv_a[j].astype(jnp.float32)
    send_b[...] = total.astype(jnp.bfloat16)
    exchange(1, 0, lambda other: send_b.at[other], lambda j: recv_b.at[j])
    total = send_b[me[1]].astype(jnp.float32)
    for j in range(sizes[1] - 1):
        total = total + recv_b[j].astype(jnp.float32)
    send_c[...] = total.astype(jnp.bfloat16)
    exchange(2, 0, lambda other: send_c.at[other], lambda j: recv_c.at[j])
    total = send_c[me[2]].astype(jnp.float32)
    for j in range(sizes[2] - 1):
        total = total + recv_c[j].astype(jnp.float32)

    row = lax.broadcasted_iota(jnp.int32, total.shape, 0)
    grad = total * jnp.where(row < rows_two, scales[0], scales[1])

    square = grad * grad
    both = jnp.sum(square, axis=0, keepdims=True)
    two = jnp.sum(jnp.where(row < rows_two, square, 0.0), axis=0, keepdims=True)
    line = lax.broadcasted_iota(jnp.int32, (8, 128), 0)
    sums = jnp.where(line == 0, two, jnp.where(line == 1, both - two, 0.0))
    first = 0
    for axis in range(3):
        sum_send[axis] = sums
        exchange(axis, 1, lambda other: sum_send.at[axis], lambda j: sum_recv.at[first + j])
        for j in range(sizes[axis] - 1):
            sums = sums + sum_recv[first + j]
        first += sizes[axis] - 1
    norm_g = jnp.sqrt(jnp.sum(sums, axis=1, keepdims=True))
    trust = TRUST * norm_ref[...] / (norm_g + EPSILON)
    rate = LEARN * jnp.where(row < rows_two, trust[0:1], trust[1:2])
    moment = MOMENTUM * m_ref[...] + rate * grad
    mom_ref[...] = moment

    all_ref[me[0], me[1], me[2]] = moment.astype(jnp.bfloat16)
    exchange(2, 2, lambda other: all_ref.at[me[0], me[1], me[2]],
             lambda j: all_ref.at[me[0], me[1], me[2]])
    exchange(1, 2, lambda other: all_ref.at[me[0], me[1]], lambda j: all_ref.at[me[0], me[1]])
    exchange(0, 2, lambda other: all_ref.at[me[0]], lambda j: all_ref.at[me[0]])


def update(part_two, part_three, weight_two, weight_three, moment_two, moment_three,
           norm_two, norm_three, scale_two, scale_three):
    sizes = tuple(lax.axis_size(name) for name in AXES)
    devices = sizes[0] * sizes[1] * sizes[2]
    shard_two, shard_three = (moment_two.shape[0], moment_three.shape[0])
    rows_two, rows_three = (-(-shard_two // 128), -(-shard_three // 128))
    rows = -(-(rows_two + rows_three) // 16) * 16

    def flat_chunks(two, three, count, dtype):
        two = two.astype(dtype).reshape(count, shard_two)
        three = three.astype(dtype).reshape(count, shard_three)
        two = jnp.pad(two, ((0, 0), (0, rows_two * 128 - shard_two)))
        three = jnp.pad(three, ((0, 0), (0, (rows - rows_two) * 128 - shard_three)))
        joined = jnp.concatenate([two, three], axis=1)
        return joined.reshape(count, rows, 128)

    grads = flat_chunks(part_two, part_three, devices, jnp.bfloat16)
    grads = grads.reshape(sizes[0], sizes[1], sizes[2], rows, 128)
    moments = flat_chunks(moment_two, moment_three, 1, jnp.float32)[0]
    norms = jnp.where(
        lax.broadcasted_iota(jnp.int32, (8, 128), 0) == 0, norm_two, norm_three
    )
    bf16, f32 = (jnp.bfloat16, jnp.float32)
    copies = 3 * sum(size - 1 for size in sizes)
    vmem = pl.BlockSpec(memory_space=pltpu.VMEM)
    own, full = pl.pallas_call(
        functools.partial(update_kernel, sizes, rows_two, (scale_two, scale_three)),
        out_shape=(
            jax.ShapeDtypeStruct((rows, 128), f32),
            jax.ShapeDtypeStruct((*sizes, rows, 128), bf16),
        ),
        in_specs=[vmem] * 3,
        out_specs=(vmem, vmem),
        scratch_shapes=[
            pltpu.VMEM((sizes[0] - 1, sizes[1], sizes[2], rows, 128), bf16),
            pltpu.VMEM((sizes[1] - 1, sizes[2], rows, 128), bf16),
            pltpu.VMEM((sizes[2] - 1, rows, 128), bf16),
            pltpu.VMEM((sizes[1], sizes[2], rows, 128), bf16),
            pltpu.VMEM((sizes[2], rows, 128), bf16),
            pltpu.VMEM((3, 8, 128), f32),
            pltpu.VMEM((copies // 3, 8, 128), f32),
            pltpu.SemaphoreType.DMA((copies,)),
            pltpu.SemaphoreType.DMA((copies,)),
        ],
        compiler_params=pltpu.CompilerParams(
            collective_id=1, has_side_effects=True, vmem_limit_bytes=32 * 2**20
        ),
        name="update",
    )(grads, moments, norms)
    own = own.reshape(-1)
    new_moment_two = own[:shard_two]
    new_moment_three = own[rows_two * 128 : rows_two * 128 + shard_three]
    full = full.reshape(devices, rows * 128)
    full_two = full[:, :shard_two].reshape(weight_two.shape).astype(f32)
    begin = rows_two * 128
    full_three = full[:, begin : begin + shard_three].reshape(weight_three.shape).astype(f32)
    return (weight_two - full_two, weight_three - full_three, new_moment_two, new_moment_three)


def local(act_one, pre_two, cot_three, weight_two, weight_three, moment_two, moment_three):
    chan_one = act_one.shape[1]
    chan_two = pre_two.shape[1]
    chan_three = cot_three.shape[1]
    local_d, local_h, local_w = (pre_two.shape[2], pre_two.shape[3], pre_two.shape[4])
    half_d, half_h, half_w = (local_d // 2, local_h // 2, local_w // 2)
    flat_len = half_h * half_w
    volumes = lax.axis_size("dp")
    scale_two = (chan_one * 27) ** (-0.5)
    scale_three = (chan_two * 27) ** (-0.5)
    pre_f = pre_two[0].astype(jnp.float32)
    pooled = leaky(pre_f).reshape(chan_two, half_d, 2, half_h, 2, half_w, 2).mean(axis=(2, 4, 6))
    pooled = pooled.astype(jnp.bfloat16).reshape(chan_two, half_d, flat_len)
    wb_three = weight_three.astype(jnp.bfloat16).reshape(chan_three, chan_two, 27)
    wb_two = weight_two.astype(jnp.bfloat16).reshape(chan_two, chan_one, 27)
    rim_depth = padded_2(cot_three, (("depth", 2),), 1)
    rim_both = padded_2(rim_depth, (("height", 3),), half_w)
    flat = jnp.pad(rim_both[0], ((0, 0), (0, 0), (1, 1)))
    column = lax.broadcasted_iota(jnp.int32, (1, 1, flat_len), 2) % half_w
    back = jnp.zeros((chan_two, half_d, flat_len), jnp.float32)
    grads_three = []
    for k in range(27):
        kd, kh, kw = (k // 9, k // 3 % 3, k % 3)
        od, oh, ow = (2 - kd, 2 - kh, 2 - kw)
        begin = oh * half_w + ow
        piece = flat[:, od : od + half_d, begin : begin + flat_len]
        inside = (column + ow - 1 >= 0) & (column + ow - 1 < half_w)
        piece = jnp.where(inside, piece, jnp.zeros_like(piece))
        back = back + jnp.einsum(
            "oi,odn->idn", wb_three[:, :, k], piece, preferred_element_type=jnp.float32
        )
        grads_three.append(
            jnp.einsum("odn,idn->oi", piece, pooled, preferred_element_type=jnp.float32)
        )
    back = (scale_three * back).astype(jnp.bfloat16).astype(jnp.float32)
    upper = jnp.broadcast_to(
        back.reshape(chan_two, half_d, 1, half_h, 1, half_w, 1),
        (chan_two, half_d, 2, half_h, 2, half_w, 2),
    )
    upper = upper.reshape(chan_two, local_d, local_h, local_w)
    cot_two = (upper * 0.125 * slope_of(pre_f)).astype(jnp.bfloat16)
    grads_two = []
    rim_fine = padded_2(cot_two[None], (("depth", 2), ("height", 3)), 1)[0]
    padded = jnp.pad(rim_fine, ((0, 0), (0, 0), (0, 0), (1, 1)))
    act_local = act_one[0]
    into = jnp.zeros((chan_one, local_d, local_h, local_w), jnp.float32)
    for k in range(27):
        kd, kh, kw = (k // 9, k // 3 % 3, k % 3)
        od, oh, ow = (2 - kd, 2 - kh, 2 - kw)
        piece = padded[:, od : od + local_d, oh : oh + local_h, ow : ow + local_w]
        into = into + jnp.einsum(
            "oi,odhw->idhw", wb_two[:, :, k], piece, preferred_element_type=jnp.float32
        )
        grads_two.append(
            jnp.einsum("odhw,idhw->oi", piece, act_local, preferred_element_type=jnp.float32)
        )
    grad_input = (scale_two * into).astype(jnp.bfloat16)[None]
    part_two = jnp.stack(grads_two, -1).reshape(chan_two, chan_one * 27)
    part_three = jnp.stack(grads_three, -1).reshape(chan_three, chan_two * 27)
    shard_two = moment_two.shape[0]
    shard_three = moment_three.shape[0]
    norm_w_two = jnp.sqrt(jnp.sum(weight_two * weight_two))
    norm_w_three = jnp.sqrt(jnp.sum(weight_three * weight_three))
    new_weight_two, new_weight_three, new_moment_two, new_moment_three = update(
        part_two, part_three, weight_two, weight_three, moment_two, moment_three,
        norm_w_two, norm_w_three, scale_two / volumes, scale_three / volumes,
    )
    return (grad_input, new_weight_two, new_weight_three, new_moment_two, new_moment_three)


def solution(mesh):
    in_specs = (
        P("dp", None, "depth", "height", None),
        P("dp", None, "depth", "height", None),
        P("dp", None, "depth", "height"),
        P(),
        P(),
        P(("dp", "depth", "height")),
        P(("dp", "depth", "height")),
    )
    out_specs = (
        P("dp", None, "depth", "height", None),
        P(),
        P(),
        P(("dp", "depth", "height")),
        P(("dp", "depth", "height")),
    )
    return jax.shard_map(local, mesh=mesh, in_specs=in_specs, out_specs=out_specs, check_vma=False)
```

```python
import functools

import jax
import jax.numpy as jnp
from jax import lax
from jax.experimental import pallas as pl
from jax.experimental.pallas import tpu as pltpu
from jax.sharding import PartitionSpec as P

AXES = ("dp", "depth", "height")
MESH = pl.DeviceIdType.MESH

SLOPE = 0.3
LEARN = 4.0
TRUST = 0.05
MOMENTUM = 0.9
EPSILON = 1e-06


def leaky(value):
    return jnp.where(value > 0, value, SLOPE * value)


def slope_of(value):
    return jnp.where(value > 0, 1.0, SLOPE).astype(jnp.float32)


def partners(sizes, me):
    out = []
    for axis, size in enumerate(sizes):
        group = []
        for step in range(1, size):
            other = lax.rem(me[axis] + step, size)
            group.append((other, tuple(other if i == axis else me[i] for i in range(3))))
        out.append(group)
    return out


def update_kernel(
    sizes, rows_two, scales, g_ref, m_ref, norm_ref, mom_ref, all_ref,
    recv_a, recv_b, recv_c, send_b, send_c, sum_send, sum_recv, send_sem, recv_sem,
):
    me = [lax.axis_index(name) for name in AXES]
    groups = partners(sizes, me)
    count = sum(size - 1 for size in sizes)
    barrier = pltpu.get_barrier_semaphore()
    for group in groups:
        for _, device in group:
            pl.semaphore_signal(barrier, inc=1, device_id=device, device_id_type=MESH)
    pl.semaphore_wait(barrier, count)

    def exchange(axis, phase, source, target):
        base = phase * count + sum(size - 1 for size in sizes[:axis])
        copies = []
        for j, (other, device) in enumerate(groups[axis]):
            copy = pltpu.make_async_remote_copy(
                src_ref=source(other),
                dst_ref=target(j),
                send_sem=send_sem.at[base + j],
                recv_sem=recv_sem.at[base + j],
                device_id=device,
                device_id_type=MESH,
            )
            copy.start()
            copies.append(copy)
        for copy in copies:
            copy.wait()

    exchange(0, 0, lambda other: g_ref.at[other], lambda j: recv_a.at[j])
    total = g_ref[me[0]].astype(jnp.float32)
    for j in range(sizes[0] - 1):
        total = total + recv_a[j].astype(jnp.float32)
    send_b[...] = total.astype(jnp.bfloat16)
    exchange(1, 0, lambda other: send_b.at[other], lambda j: recv_b.at[j])
    total = send_b[me[1]].astype(jnp.float32)
    for j in range(sizes[1] - 1):
        total = total + recv_b[j].astype(jnp.float32)
    send_c[...] = total.astype(jnp.bfloat16)
    exchange(2, 0, lambda other: send_c.at[other], lambda j: recv_c.at[j])
    total = send_c[me[2]].astype(jnp.float32)
    for j in range(sizes[2] - 1):
        total = total + recv_c[j].astype(jnp.float32)

    row = lax.broadcasted_iota(jnp.int32, total.shape, 0)
    grad = total * jnp.where(row < rows_two, scales[0], scales[1])

    square = grad * grad
    both = jnp.sum(square, axis=0, keepdims=True)
    two = jnp.sum(jnp.where(row < rows_two, square, 0.0), axis=0, keepdims=True)
    line = lax.broadcasted_iota(jnp.int32, (8, 128), 0)
    sums = jnp.where(line == 0, two, jnp.where(line == 1, both - two, 0.0))
    first = 0
    for axis in range(3):
        sum_send[axis] = sums
        exchange(axis, 1, lambda other: sum_send.at[axis], lambda j: sum_recv.at[first + j])
        for j in range(sizes[axis] - 1):
            sums = sums + sum_recv[first + j]
        first += sizes[axis] - 1
    norm_g = jnp.sqrt(jnp.sum(sums, axis=1, keepdims=True))
    trust = TRUST * norm_ref[...] / (norm_g + EPSILON)
    rate = LEARN * jnp.where(row < rows_two, trust[0:1], trust[1:2])
    moment = MOMENTUM * m_ref[...] + rate * grad
    mom_ref[...] = moment

    all_ref[me[0], me[1], me[2]] = moment.astype(jnp.bfloat16)
    exchange(2, 2, lambda other: all_ref.at[me[0], me[1], me[2]],
             lambda j: all_ref.at[me[0], me[1], me[2]])
    exchange(1, 2, lambda other: all_ref.at[me[0], me[1]], lambda j: all_ref.at[me[0], me[1]])
    exchange(0, 2, lambda other: all_ref.at[me[0]], lambda j: all_ref.at[me[0]])


def update(part_two, part_three, weight_two, weight_three, moment_two, moment_three,
           norm_two, norm_three, scale_two, scale_three):
    sizes = tuple(lax.axis_size(name) for name in AXES)
    devices = sizes[0] * sizes[1] * sizes[2]
    shard_two, shard_three = (moment_two.shape[0], moment_three.shape[0])
    rows_two, rows_three = (-(-shard_two // 128), -(-shard_three // 128))
    rows = -(-(rows_two + rows_three) // 16) * 16

    def flat_chunks(two, three, count, dtype):
        two = two.astype(dtype).reshape(count, shard_two)
        three = three.astype(dtype).reshape(count, shard_three)
        two = jnp.pad(two, ((0, 0), (0, rows_two * 128 - shard_two)))
        three = jnp.pad(three, ((0, 0), (0, (rows - rows_two) * 128 - shard_three)))
        joined = jnp.concatenate([two, three], axis=1)
        return joined.reshape(count, rows, 128)

    grads = flat_chunks(part_two, part_three, devices, jnp.bfloat16)
    grads = grads.reshape(sizes[0], sizes[1], sizes[2], rows, 128)
    moments = flat_chunks(moment_two, moment_three, 1, jnp.float32)[0]
    norms = jnp.where(
        lax.broadcasted_iota(jnp.int32, (8, 128), 0) == 0, norm_two, norm_three
    )
    bf16, f32 = (jnp.bfloat16, jnp.float32)
    copies = 3 * sum(size - 1 for size in sizes)
    vmem = pl.BlockSpec(memory_space=pltpu.VMEM)
    own, full = pl.pallas_call(
        functools.partial(update_kernel, sizes, rows_two, (scale_two, scale_three)),
        out_shape=(
            jax.ShapeDtypeStruct((rows, 128), f32),
            jax.ShapeDtypeStruct((*sizes, rows, 128), bf16),
        ),
        in_specs=[vmem] * 3,
        out_specs=(vmem, vmem),
        scratch_shapes=[
            pltpu.VMEM((sizes[0] - 1, sizes[1], sizes[2], rows, 128), bf16),
            pltpu.VMEM((sizes[1] - 1, sizes[2], rows, 128), bf16),
            pltpu.VMEM((sizes[2] - 1, rows, 128), bf16),
            pltpu.VMEM((sizes[1], sizes[2], rows, 128), bf16),
            pltpu.VMEM((sizes[2], rows, 128), bf16),
            pltpu.VMEM((3, 8, 128), f32),
            pltpu.VMEM((copies // 3, 8, 128), f32),
            pltpu.SemaphoreType.DMA((copies,)),
            pltpu.SemaphoreType.DMA((copies,)),
        ],
        compiler_params=pltpu.CompilerParams(
            collective_id=1, has_side_effects=True, vmem_limit_bytes=32 * 2**20
        ),
        name="update",
    )(grads, moments, norms)
    own = own.reshape(-1)
    new_moment_two = own[:shard_two]
    new_moment_three = own[rows_two * 128 : rows_two * 128 + shard_three]
    full = full.reshape(devices, rows * 128)
    full_two = full[:, :shard_two].reshape(weight_two.shape).astype(f32)
    begin = rows_two * 128
    full_three = full[:, begin : begin + shard_three].reshape(weight_three.shape).astype(f32)
    return (weight_two - full_two, weight_three - full_three, new_moment_two, new_moment_three)


def halo_kernel(widths, cot_ref, pre_ref, cot_out, pre_out, send_sem, recv_sem, own_sem):
    me = [lax.axis_index(name) for name in AXES]
    last = [lax.axis_size(name) - 1 for name in AXES]
    sides = [(d, h) for d in (-1, 0, 1) for h in (-1, 0, 1) if (d, h) != (0, 0)]

    def present(d, h):
        depth, height = (me[1] + d, me[2] + h)
        return (depth >= 0) & (depth <= last[1]) & (height >= 0) & (height <= last[2])

    def part(side, length, width, taken):
        if side == 0:
            return pl.ds(0 if taken else width, length)
        if taken:
            return pl.ds(length - width if side > 0 else 0, width)
        return pl.ds(0 if side > 0 else width + length, width)

    arrays = ((cot_ref, cot_out, widths[0]), (pre_ref, pre_out, widths[1]))

    def place(ref, width, d, h, taken):
        layers, _, lanes = ref.shape
        return (part(d, layers, width[0], taken), slice(None), part(h, lanes, width[1], taken))

    barrier = pltpu.get_barrier_semaphore()
    for d, h in sides:
        @pl.when(present(d, h))
        def _():
            pl.semaphore_signal(
                barrier, inc=1, device_id=(me[0], me[1] + d, me[2] + h), device_id_type=MESH
            )
    along = [
        jnp.where(me[i] > 0, 1, 0) + jnp.where(me[i] < last[i], 1, 0) + 1 for i in (1, 2)
    ]
    pl.semaphore_wait(barrier, along[0] * along[1] - 1)

    def remote(n, a, d, h):
        ref, out, width = arrays[a]
        return pltpu.make_async_remote_copy(
            src_ref=ref.at[place(ref, width, d, h, True)],
            dst_ref=out.at[place(ref, width, d, h, False)],
            send_sem=send_sem.at[2 * n + a],
            recv_sem=recv_sem.at[2 * n + a],
            device_id=(me[0], me[1] + d, me[2] + h),
            device_id_type=MESH,
        )

    for n, (d, h) in enumerate(sides):
        @pl.when(present(d, h))
        def _():
            for a in range(2):
                remote(n, a, d, h).start()
    own = []
    for a, (ref, out, width) in enumerate(arrays):
        copy = pltpu.make_async_copy(ref, out.at[place(ref, width, 0, 0, False)], own_sem.at[a])
        copy.start()
        own.append(copy)
    for d, h in sides:
        @pl.when(jnp.logical_not(present(-d, -h)))
        def _():
            for ref, out, width in arrays:
                where = place(ref, width, d, h, False)
                shape = (where[0].size, ref.shape[1], where[2].size)
                out[where] = jnp.zeros(shape, out.dtype)
    for copy in own:
        copy.wait()
    for n, (d, h) in enumerate(sides):
        @pl.when(present(d, h))
        def _():
            for a in range(2):
                remote(n, a, d, h).wait_send()

        @pl.when(present(-d, -h))
        def _():
            for a in range(2):
                remote(n, a, d, h).wait_recv()


def with_halo(cot, pre, lanes_cot, lanes_pre):
    widths = ((2, lanes_cot), (1, lanes_pre))
    out_shape = tuple(
        jax.ShapeDtypeStruct((x.shape[0] + 2 * d, x.shape[1], x.shape[2] + 2 * n), x.dtype)
        for x, (d, n) in zip((cot, pre), widths)
    )
    vmem = pl.BlockSpec(memory_space=pltpu.VMEM)
    return pl.pallas_call(
        functools.partial(halo_kernel, widths),
        out_shape=out_shape,
        in_specs=[vmem] * 2,
        out_specs=(vmem, vmem),
        scratch_shapes=[
            pltpu.SemaphoreType.DMA((16,)),
            pltpu.SemaphoreType.DMA((16,)),
            pltpu.SemaphoreType.DMA((2,)),
        ],
        compiler_params=pltpu.CompilerParams(
            collective_id=0, has_side_effects=True, vmem_limit_bytes=32 * 2**20
        ),
        name="halo",
    )(cot, pre)


def dot(a, b):
    return jnp.dot(a, b, preferred_element_type=jnp.float32)


def dot_t(a, b):
    return lax.dot_general(a, b, (((1,), (1,)), ((), ())), preferred_element_type=jnp.float32)


def conv_kernel(
    half_w, scales, cot_ref, pre_ref, act_ref, w2_ref, w3_ref, gin_ref, g2_ref, g3_ref,
    perm3, perm2, wide3, wide2, taps3, taps2, back_acc, upper, act_wide, pool_wide, into,
):
    bf16, f32 = (jnp.bfloat16, jnp.float32)
    chan_three, chan_two, chan_one = (cot_ref.shape[1], pre_ref.shape[1], act_ref.shape[1])
    wide = 2 * half_w
    layers3, lanes3 = (cot_ref.shape[0], cot_ref.shape[2])
    inner3 = lanes3 - wide
    layers2, lanes2 = (pre_ref.shape[0], pre_ref.shape[2])
    own_layers, own_lanes = act_ref.shape[0], act_ref.shape[2]
    rows2 = lanes2 // wide
    iota = lambda shape, dim: lax.broadcasted_iota(jnp.int32, shape, dim)
    depth, height = (lax.axis_index("depth"), lax.axis_index("height"))
    one = lambda flag: jnp.where(flag, 1.0, 0.0).astype(f32)
    above, below = (one(depth > 0), one(depth < lax.axis_size("depth") - 1))
    left, right = (one(height > 0), one(height < lax.axis_size("height") - 1))

    n3, n2 = (3 * chan_two, 3 * chan_one)
    row3, col3 = (iota((n3, 1), 0), iota((1, 27 * chan_two), 1))
    row2, col2 = (iota((n2, 1), 0), iota((1, 27 * chan_one), 1))
    for t in range(9):
        aim = (row3 % chan_two) * 27 + (row3 // chan_two) * 9 + t
        perm3[t] = jnp.where(col3 == aim, 1.0, 0.0).astype(bf16)
        aim = (row2 % chan_one) * 27 + (t // 3) * 9 + (row2 // chan_one) * 3 + t % 3
        perm2[t] = jnp.where(col2 == aim, 1.0, 0.0).astype(bf16)
    w3, w2 = (w3_ref[...].astype(bf16), w2_ref[...].astype(bf16))
    for t in range(9):
        taps3[:, t * chan_three : (t + 1) * chan_three] = dot_t(perm3[t], w3).astype(bf16)
    for kd in range(3):
        taps2[kd * n2 : (kd + 1) * n2, :] = jnp.concatenate(
            [dot_t(perm2[kd * 3 + kw], w2) for kw in range(3)], axis=1
        ).astype(bf16)

    back_acc[...] = jnp.zeros_like(back_acc)
    column3 = iota((1, lanes3), 1) % half_w

    @pl.loop(0, layers3)
    def _(e):
        whole = cot_ref[e].astype(f32)
        for kw in range(3):
            ow = 2 - kw
            moved = whole
            if ow == 0:
                moved = jnp.where(column3 == 0, 0.0, pltpu.roll(whole, 1, 1))
            elif ow == 2:
                moved = jnp.where(column3 == half_w - 1, 0.0, pltpu.roll(whole, lanes3 - 1, 1))
            for kh in range(3):
                start = (2 - kh) * half_w
                piece = moved if start == 0 else pltpu.roll(moved, lanes3 - start, 1)
                t = kh * 3 + kw
                wide3[e, t * chan_three : (t + 1) * chan_three, :] = piece[:, :inner3].astype(bf16)
        product = dot(taps3[...], wide3[e])
        for kd in range(3):
            back_acc[e + kd] += product[kd * chan_two : (kd + 1) * chan_two]

    twice = jnp.where(iota((wide, 2 * wide), 0) == iota((wide, 2 * wide), 1) // 2, 1.0, 0.0)
    twice = twice.astype(bf16)
    for layer in range(layers3 - 2):
        cells = (scales[1] * back_acc[layer + 2]).astype(bf16)
        for pair in range(inner3 // wide):
            upper[layer, :, pair * 2 * wide : (pair + 1) * 2 * wide] = dot(
                cells[:, pair * wide : (pair + 1) * wide], twice
            )

    halves = jnp.where(iota((2 * wide, wide), 0) // 2 == iota((2 * wide, wide), 1), 0.125, 0.0)
    halves = halves.astype(bf16)
    coarse = own_layers // 2
    pool_wide[...] = jnp.zeros_like(pool_wide)
    for d in range(coarse):
        total = leaky(pre_ref[2 * d + 1].astype(f32)) + leaky(pre_ref[2 * d + 2].astype(f32))
        coarse_rows = inner3 // half_w
        sums = []
        for q in range(coarse_rows):
            if q in (0, coarse_rows - 1):
                sums.append(jnp.zeros((chan_two, wide), f32))
            else:
                at = (2 * q - 1) * wide
                sums.append(total[:, at : at + wide] + total[:, at + wide : at + 2 * wide])
        for pair in range(coarse_rows // 2):
            both = jnp.concatenate(sums[2 * pair : 2 * pair + 2], axis=1)
            high = both.astype(bf16)
            low = (both - high.astype(f32)).astype(bf16)
            mean = (dot(high, halves) + dot(low, halves)).astype(bf16)
            for kd in range(3):
                pool_wide[
                    d + 2 - kd, kd * chan_two : (kd + 1) * chan_two, pair * wide : (pair + 1) * wide
                ] = mean

    for t in range(9):
        rows = slice(t * chan_three, (t + 1) * chan_three)
        grad = dot_t(wide3[1, rows, :], pool_wide[0])
        for e in range(1, coarse + 2):
            grad = grad + dot_t(wide3[e + 1, rows, :], pool_wide[e])
        ordered = dot(grad.astype(bf16), perm3[t])
        if t == 0:
            g3_ref[...] = ordered
        else:
            g3_ref[...] += ordered

    column2 = iota((1, lanes2), 1) % wide
    lane = iota((1, lanes2), 1)
    edge = jnp.where(lane < wide, left, jnp.where(lane >= lanes2 - wide, right, 1.0))
    into[...] = jnp.zeros_like(into)

    @pl.loop(0, layers2)
    def _(f):
        parent = upper[(f + 1) // 2]
        cells = [parent[:, (r + 1) // 2 * wide : ((r + 1) // 2 + 1) * wide] for r in range(rows2)]
        spread = jnp.concatenate(cells, axis=1)
        inside = edge * jnp.where(f == 0, above, jnp.where(f == layers2 - 1, below, 1.0))
        value = spread * 0.125 * slope_of(pre_ref[f].astype(f32))
        value = jnp.where(inside > 0, value, 0.0)
        before = jnp.where(column2 == 0, 0.0, pltpu.roll(value, 1, 1))
        after = jnp.where(column2 == wide - 1, 0.0, pltpu.roll(value, lanes2 - 1, 1))
        for kw, moved in enumerate((after, value, before)):
            wide2[f, kw * chan_two : (kw + 1) * chan_two, :] = moved.astype(bf16)
        product = dot(taps2[...], wide2[f])
        for kd in range(3):
            total = None
            for kh in range(3):
                at, start = ((kd * 3 + kh) * chan_one, (2 - kh) * wide)
                term = product[at : at + chan_one, start : start + own_lanes]
                total = term if total is None else total + term
            into[f + kd] += total

    for d in range(own_layers):
        gin_ref[d] = (scales[0] * into[d + 2]).astype(bf16)

    act_wide[...] = jnp.zeros_like(act_wide)
    for d in range(own_layers):
        for kh in range(3):
            start = (2 - kh) * wide
            act_wide[d, kh * chan_one : (kh + 1) * chan_one, start : start + own_lanes] = act_ref[d]
    n_wide = 3 * chan_two
    for kd in range(3):
        grad = dot_t(wide2[2 - kd], act_wide[0])
        for d in range(1, own_layers):
            grad = grad + dot_t(wide2[d + 2 - kd], act_wide[d])
        grad = grad.astype(bf16)
        for kw in range(3):
            ordered = dot(grad[kw * chan_two : (kw + 1) * chan_two], perm2[kd * 3 + kw])
            if kd == 0 and kw == 0:
                g2_ref[...] = ordered
            else:
                g2_ref[...] += ordered


def local(act_one, pre_two, cot_three, weight_two, weight_three, moment_two, moment_three):
    chan_one, chan_two, chan_three = (act_one.shape[1], pre_two.shape[1], cot_three.shape[1])
    local_d, local_h, local_w = pre_two.shape[2:]
    half_w = local_w // 2
    volumes = lax.axis_size("dp")
    scale_two = (chan_one * 27) ** (-0.5)
    scale_three = (chan_two * 27) ** (-0.5)
    bf16, f32 = (jnp.bfloat16, jnp.float32)

    def by_layer(x):
        return x[0].reshape(x.shape[1], x.shape[2], -1).transpose(1, 0, 2)

    act = by_layer(act_one)
    cot, pre = with_halo(by_layer(cot_three), by_layer(pre_two), 2 * half_w, local_w)
    layers3, _, lanes3 = cot.shape
    layers2, _, lanes2 = pre.shape
    inner3 = lanes3 - 2 * half_w
    vmem = pl.BlockSpec(memory_space=pltpu.VMEM)
    grad_input, part_two, part_three = pl.pallas_call(
        functools.partial(conv_kernel, half_w, (scale_two, scale_three)),
        out_shape=(
            jax.ShapeDtypeStruct(act.shape, bf16),
            jax.ShapeDtypeStruct(weight_two.shape, f32),
            jax.ShapeDtypeStruct(weight_three.shape, f32),
        ),
        in_specs=[vmem] * 5,
        out_specs=(vmem,) * 3,
        scratch_shapes=[
            pltpu.VMEM((9, 3 * chan_two, 27 * chan_two), bf16),
            pltpu.VMEM((9, 3 * chan_one, 27 * chan_one), bf16),
            pltpu.VMEM((layers3, 9 * chan_three, inner3), bf16),
            pltpu.VMEM((layers2, 3 * chan_two, lanes2), bf16),
            pltpu.VMEM((3 * chan_two, 9 * chan_three), bf16),
            pltpu.VMEM((9 * chan_one, 3 * chan_two), bf16),
            pltpu.VMEM((layers3 + 2, chan_two, inner3), f32),
            pltpu.VMEM((layers3 - 2, chan_two, 2 * inner3), f32),
            pltpu.VMEM((local_d, 3 * chan_one, lanes2), bf16),
            pltpu.VMEM((local_d // 2 + 2, 3 * chan_two, inner3), bf16),
            pltpu.VMEM((layers2 + 2, chan_one, act.shape[2]), f32),
        ],
        compiler_params=pltpu.CompilerParams(vmem_limit_bytes=56 * 2**20),
        name="convolutions",
    )(cot, pre, act, weight_two, weight_three)
    grad_input = grad_input.transpose(1, 0, 2).reshape(act_one.shape)
    norm_w_two = jnp.sqrt(jnp.sum(weight_two * weight_two))
    norm_w_three = jnp.sqrt(jnp.sum(weight_three * weight_three))
    new_weight_two, new_weight_three, new_moment_two, new_moment_three = update(
        part_two, part_three, weight_two, weight_three, moment_two, moment_three,
        norm_w_two, norm_w_three, scale_two / volumes, scale_three / volumes,
    )
    return (grad_input, new_weight_two, new_weight_three, new_moment_two, new_moment_three)


def solution(mesh):
    in_specs = (
        P("dp", None, "depth", "height", None),
        P("dp", None, "depth", "height", None),
        P("dp", None, "depth", "height"),
        P(),
        P(),
        P(("dp", "depth", "height")),
        P(("dp", "depth", "height")),
    )
    out_specs = (
        P("dp", None, "depth", "height", None),
        P(),
        P(),
        P(("dp", "depth", "height")),
        P(("dp", "depth", "height")),
    )
    return jax.shard_map(local, mesh=mesh, in_specs=in_specs, out_specs=out_specs, check_vma=False)
```

```python
import functools

import jax
import jax.numpy as jnp
from jax import lax
from jax.experimental import pallas as pl
from jax.experimental.pallas import tpu as pltpu
from jax.sharding import PartitionSpec as P

AXES = ("dp", "depth", "height")
MESH = pl.DeviceIdType.MESH

SLOPE = 0.3
LEARN = 4.0
TRUST = 0.05
MOMENTUM = 0.9
EPSILON = 1e-06


def leaky(value):
    return jnp.where(value > 0, value, SLOPE * value)


def slope_of(value):
    return jnp.where(value > 0, 1.0, SLOPE).astype(jnp.float32)


def dot(a, b):
    return jnp.dot(a, b, preferred_element_type=jnp.float32)


def dot_t(a, b):
    return lax.dot_general(a, b, (((1,), (1,)), ((), ())), preferred_element_type=jnp.float32)


def step_kernel(
    half_w, scales, rates, cot_ref, pre_ref, act_ref, w2_ref, w3_ref, m2_ref, m3_ref,
    gin_ref, new2_ref, new3_ref, mom2_ref, mom3_ref,
    cot_x, pre_x, perm3, perm2, wide3, wide2, taps3, taps2, back_acc, upper, act_wide, pool_wide,
    into, g2_acc, g3_acc, squared, *rest,
):
    layer_refs, (send_sem, recv_sem, own_sem) = (rest[:-3], rest[-3:])
    per_layer = len(layer_refs) // 2
    names = ("parts", "recv_a", "send_b", "recv_b", "send_c", "recv_c", "moments", "full")
    layer2 = dict(zip(names, layer_refs[:per_layer]))
    layer3 = dict(zip(names, layer_refs[per_layer:]))
    me = [lax.axis_index(name) for name in AXES]
    sizes = [lax.axis_size(name) for name in AXES]
    last = [size - 1 for size in sizes]
    used = [0]

    def device(axis, index):
        return tuple(index if i == axis else me[i] for i in range(3))

    def others(axis):
        return [lax.rem(me[axis] + step, sizes[axis]) for step in range(1, sizes[axis])]

    def remote(source, target, to):
        n = used[0]
        used[0] += 1
        return pltpu.make_async_remote_copy(
            src_ref=source, dst_ref=target, send_sem=send_sem.at[n], recv_sem=recv_sem.at[n],
            device_id=to, device_id_type=MESH,
        )

    def send(axis, source, target):
        copies = []
        for j, other in enumerate(others(axis)):
            copy = remote(source(other), target(j), device(axis, other))
            copy.start()
            copies.append(copy)
        return copies

    def finish(copies):
        for copy in copies:
            copy.wait()

    sides = [(d, h) for d in (-1, 0, 1) for h in (-1, 0, 1) if (d, h) != (0, 0)]

    def present(d, h):
        down, along = (me[1] + d, me[2] + h)
        return (down >= 0) & (down <= last[1]) & (along >= 0) & (along <= last[2])

    def part(side, length, width, taken):
        if side == 0:
            return pl.ds(0 if taken else width, length)
        if taken:
            return pl.ds(length - width if side > 0 else 0, width)
        return pl.ds(0 if side > 0 else width + length, width)

    arrays = ((cot_ref, cot_x, (2, 2 * half_w)), (pre_ref, pre_x, (1, 2 * half_w)))

    def place(ref, width, d, h, taken):
        layers, _, lanes = ref.shape
        return (part(d, layers, width[0], taken), slice(None), part(h, lanes, width[1], taken))

    barrier = pltpu.get_barrier_semaphore()

    def greet(to):
        pl.semaphore_signal(barrier, inc=1, device_id=to, device_id_type=MESH)

    for i in range(sizes[0]):
        for j in range(sizes[1]):
            if i or j:
                a, b = (lax.rem(me[0] + i, sizes[0]), lax.rem(me[1] + j, sizes[1]))
                greet((a, b, me[2]))
    for other in others(2):
        greet(device(2, other))
    for d, h in sides:
        if d and h:
            @pl.when(present(d, h))
            def _():
                greet((me[0], me[1] + d, me[2] + h))
    around = [jnp.where(me[i] > 0, 1, 0) + jnp.where(me[i] < last[i], 1, 0) for i in (1, 2)]
    pl.semaphore_wait(barrier, sizes[0] * sizes[1] + sizes[2] - 2 + around[0] * around[1])

    edges = [[], []]
    for a, (ref, out, width) in enumerate(arrays):
        for d, h in sides:
            copy = remote(
                ref.at[place(ref, width, d, h, True)], out.at[place(ref, width, d, h, False)],
                (me[0], me[1] + d, me[2] + h),
            )
            edges[a].append((d, h, copy))

            @pl.when(present(d, h))
            def _():
                copy.start()

    own = []
    for a, (ref, out, width) in enumerate(arrays):
        copy = pltpu.make_async_copy(ref, out.at[place(ref, width, 0, 0, False)], own_sem.at[a])
        copy.start()
        own.append(copy)
    moment_copies = []
    for layer, ref in ((layer2, m2_ref), (layer3, m3_ref)):
        layer["moments"][me[2]] = ref[...]
        moment_copies += send(
            2, lambda other: ref, lambda j: layer["moments"].at[me[2]]
        )
    for d, h in sides:
        @pl.when(jnp.logical_not(present(-d, -h)))
        def _():
            for ref, out, width in arrays:
                where = place(ref, width, d, h, False)
                shape = (where[0].size, ref.shape[1], where[2].size)
                out[where] = jnp.zeros(shape, out.dtype)

    def finish_edges(a):
        own[a].wait()
        for d, h, copy in edges[a]:
            @pl.when(present(d, h))
            def _():
                copy.wait_send()

            @pl.when(present(-d, -h))
            def _():
                copy.wait_recv()

    bf16, f32 = (jnp.bfloat16, jnp.float32)
    chan_three, chan_two, chan_one = (cot_x.shape[1], pre_x.shape[1], act_ref.shape[1])
    wide = 2 * half_w
    layers3, lanes3 = (cot_x.shape[0], cot_x.shape[2])
    inner3 = lanes3 - wide
    layers2, lanes2 = (pre_x.shape[0], pre_x.shape[2])
    own_layers, own_lanes = act_ref.shape[0], act_ref.shape[2]
    rows2 = lanes2 // wide
    iota = lambda shape, dim: lax.broadcasted_iota(jnp.int32, shape, dim)
    depth, height = (me[1], me[2])
    one = lambda flag: jnp.where(flag, 1.0, 0.0).astype(f32)
    above, below = (one(depth > 0), one(depth < sizes[1] - 1))
    left, right = (one(height > 0), one(height < sizes[2] - 1))

    n3, n2 = (3 * chan_two, 3 * chan_one)
    row3, col3 = (iota((n3, 1), 0), iota((1, 27 * chan_two), 1))
    row2, col2 = (iota((n2, 1), 0), iota((1, 27 * chan_one), 1))
    for t in range(9):
        aim = (row3 % chan_two) * 27 + (row3 // chan_two) * 9 + t
        perm3[t] = jnp.where(col3 == aim, 1.0, 0.0).astype(bf16)
        aim = (row2 % chan_one) * 27 + (t // 3) * 9 + (row2 // chan_one) * 3 + t % 3
        perm2[t] = jnp.where(col2 == aim, 1.0, 0.0).astype(bf16)
    w3, w2 = (w3_ref[...].astype(bf16), w2_ref[...].astype(bf16))
    for t in range(9):
        taps3[:, t * chan_three : (t + 1) * chan_three] = dot_t(perm3[t], w3).astype(bf16)
    for kd in range(3):
        taps2[kd * n2 : (kd + 1) * n2, :] = jnp.concatenate(
            [dot_t(perm2[kd * 3 + kw], w2) for kw in range(3)], axis=1
        ).astype(bf16)

    norms = [
        jnp.sqrt(jnp.sum(jnp.sum(w * w, axis=0, keepdims=True), axis=1, keepdims=True))
        for w in (w2_ref[...], w3_ref[...])
    ]
    halves = jnp.where(iota((2 * wide, wide), 0) // 2 == iota((2 * wide, wide), 1), 0.125, 0.0)
    halves = halves.astype(bf16)
    coarse = own_layers // 2
    pool_wide[...] = jnp.zeros_like(pool_wide)
    for d in range(coarse):
        total = leaky(pre_ref[2 * d].astype(f32)) + leaky(pre_ref[2 * d + 1].astype(f32))
        coarse_rows = inner3 // half_w
        sums = []
        for q in range(coarse_rows):
            if q in (0, coarse_rows - 1):
                sums.append(jnp.zeros((chan_two, wide), f32))
            else:
                at = (2 * q - 2) * wide
                sums.append(total[:, at : at + wide] + total[:, at + wide : at + 2 * wide])
        for pair in range(coarse_rows // 2):
            both = jnp.concatenate(sums[2 * pair : 2 * pair + 2], axis=1)
            high = both.astype(bf16)
            low = (both - high.astype(f32)).astype(bf16)
            mean = (dot(high, halves) + dot(low, halves)).astype(bf16)
            for kd in range(3):
                pool_wide[
                    d + 2 - kd, kd * chan_two : (kd + 1) * chan_two, pair * wide : (pair + 1) * wide
                ] = mean

    finish_edges(0)

    back_acc[...] = jnp.zeros_like(back_acc)
    column3 = iota((1, lanes3), 1) % half_w

    @pl.loop(0, layers3)
    def _(e):
        whole = cot_x[e].astype(f32)
        for kw in range(3):
            ow = 2 - kw
            moved = whole
            if ow == 0:
                moved = jnp.where(column3 == 0, 0.0, pltpu.roll(whole, 1, 1))
            elif ow == 2:
                moved = jnp.where(column3 == half_w - 1, 0.0, pltpu.roll(whole, lanes3 - 1, 1))
            for kh in range(3):
                start = (2 - kh) * half_w
                piece = moved if start == 0 else pltpu.roll(moved, lanes3 - start, 1)
                t = kh * 3 + kw
                wide3[e, t * chan_three : (t + 1) * chan_three, :] = piece[:, :inner3].astype(bf16)
        product = dot(taps3[...], wide3[e])
        for kd in range(3):
            back_acc[e + kd] += product[kd * chan_two : (kd + 1) * chan_two]

    twice = jnp.where(iota((wide, 2 * wide), 0) == iota((wide, 2 * wide), 1) // 2, 1.0, 0.0)
    twice = twice.astype(bf16)
    for layer in range(layers3 - 2):
        cells = (scales[1] * back_acc[layer + 2]).astype(bf16)
        for pair in range(inner3 // wide):
            upper[layer, :, pair * 2 * wide : (pair + 1) * 2 * wide] = dot(
                cells[:, pair * wide : (pair + 1) * wide], twice
            )

    for t in range(9):
        rows = slice(t * chan_three, (t + 1) * chan_three)
        grad = dot_t(wide3[1, rows, :], pool_wide[0])
        for e in range(1, coarse + 2):
            grad = grad + dot_t(wide3[e + 1, rows, :], pool_wide[e])
        ordered = dot(grad.astype(bf16), perm3[t])
        if t == 0:
            g3_acc[...] = ordered
        else:
            g3_acc[...] += ordered

    def first_sum(layer, acc):
        parts = layer["parts"]
        rows = parts.shape[2]
        for i in range(sizes[0]):
            for j in range(sizes[1]):
                at = (i * sizes[1] + j) * rows
                parts[i, j] = acc[at : at + rows].astype(bf16)
        return send(0, lambda other: parts.at[other], lambda j: layer["recv_a"].at[j])

    def second_sum(layer, copies):
        finish(copies)
        total = layer["parts"][me[0]].astype(f32)
        for j in range(sizes[0] - 1):
            total = total + layer["recv_a"][j].astype(f32)
        layer["send_b"][...] = total.astype(bf16)
        return send(
            1, lambda other: layer["send_b"].at[other], lambda j: layer["recv_b"].at[j]
        )

    def third_sum(layer, copies):
        finish(copies)
        total = layer["send_b"][me[1]].astype(f32)
        for j in range(sizes[1] - 1):
            total = total + layer["recv_b"][j].astype(f32)
        layer["send_c"][...] = total.astype(bf16)
        layer["recv_c"][me[2]] = layer["send_c"][...]
        return send(2, lambda other: layer["send_c"], lambda j: layer["recv_c"].at[me[2]])

    def summed(layer, copies, rate):
        finish(copies)
        total = layer["recv_c"][0].astype(f32)
        for j in range(1, sizes[2]):
            total = total + layer["recv_c"][j].astype(f32)
        return total * rate

    copies3 = first_sum(layer3, g3_acc)
    finish_edges(1)

    column2 = iota((1, lanes2), 1) % wide
    lane = iota((1, lanes2), 1)
    edge = jnp.where(lane < wide, left, jnp.where(lane >= lanes2 - wide, right, 1.0))
    into[...] = jnp.zeros_like(into)

    @pl.loop(0, layers2)
    def _(f):
        parent = upper[(f + 1) // 2]
        cells = [parent[:, (r + 1) // 2 * wide : ((r + 1) // 2 + 1) * wide] for r in range(rows2)]
        spread = jnp.concatenate(cells, axis=1)
        inside = edge * jnp.where(f == 0, above, jnp.where(f == layers2 - 1, below, 1.0))
        value = spread * 0.125 * slope_of(pre_x[f].astype(f32))
        value = jnp.where(inside > 0, value, 0.0)
        before = jnp.where(column2 == 0, 0.0, pltpu.roll(value, 1, 1))
        after = jnp.where(column2 == wide - 1, 0.0, pltpu.roll(value, lanes2 - 1, 1))
        for kw, moved in enumerate((after, value, before)):
            wide2[f, kw * chan_two : (kw + 1) * chan_two, :] = moved.astype(bf16)
        product = dot(taps2[...], wide2[f])
        for kd in range(3):
            total = None
            for kh in range(3):
                at, start = ((kd * 3 + kh) * chan_one, (2 - kh) * wide)
                term = product[at : at + chan_one, start : start + own_lanes]
                total = term if total is None else total + term
            into[f + kd] += total

    copies3 = second_sum(layer3, copies3)

    act_wide[...] = jnp.zeros_like(act_wide)
    for d in range(own_layers):
        for kh in range(3):
            start = (2 - kh) * wide
            act_wide[d, kh * chan_one : (kh + 1) * chan_one, start : start + own_lanes] = act_ref[d]
    n_wide = 3 * chan_two
    for kd in range(3):
        grad = dot_t(wide2[2 - kd], act_wide[0])
        for d in range(1, own_layers):
            grad = grad + dot_t(wide2[d + 2 - kd], act_wide[d])
        grad = grad.astype(bf16)
        for kw in range(3):
            ordered = dot(grad[kw * chan_two : (kw + 1) * chan_two], perm2[kd * 3 + kw])
            if kd == 0 and kw == 0:
                g2_acc[...] = ordered
            else:
                g2_acc[...] += ordered

    copies2 = first_sum(layer2, g2_acc)
    copies3 = third_sum(layer3, copies3)
    for d in range(own_layers):
        gin_ref[d] = (scales[0] * into[d + 2]).astype(bf16)
    finish(moment_copies)
    copies2 = second_sum(layer2, copies2)
    grad_three = summed(layer3, copies3, rates[1])
    copies2 = third_sum(layer2, copies2)
    grad_two = summed(layer2, copies2, rates[0])

    squares = [
        jnp.sum(jnp.sum(g * g, axis=0, keepdims=True), axis=1, keepdims=True)
        for g in (grad_two, grad_three)
    ]
    line = lax.broadcasted_iota(jnp.int32, (8, 128), 0)
    slot = me[0] * sizes[1] + me[1]
    squared[slot] = jnp.where(line == 0, squares[0], squares[1])
    copies = []
    for i in range(sizes[0]):
        for j in range(sizes[1]):
            if i or j:
                a, b = (lax.rem(me[0] + i, sizes[0]), lax.rem(me[1] + j, sizes[1]))
                copy = remote(squared.at[slot], squared.at[slot], (a, b, me[2]))
                copy.start()
                copies.append(copy)
    finish(copies)
    total = squared[0]
    for n in range(1, sizes[0] * sizes[1]):
        total = total + squared[n]
    norm_g = jnp.sqrt(total)
    copies = []
    layers = ((layer2, grad_two, mom2_ref), (layer3, grad_three, mom3_ref))
    for n, (layer, grad, mom_ref) in enumerate(layers):
        trust = TRUST * norms[n] / (norm_g[n : n + 1, 0:1] + EPSILON)
        pieces = [layer["moments"][c] for c in range(sizes[2])]
        split = grad.shape[1] // pieces[0].shape[1]
        lines = [
            pieces[c] if split == 1 else jnp.concatenate(pieces[c : c + split], axis=1)
            for c in range(0, sizes[2], split)
        ]
        old = lines[0] if len(lines) == 1 else jnp.concatenate(lines, axis=0)
        moment = MOMENTUM * old + LEARN * trust * grad
        mom_ref[...] = moment
        full = layer["full"]
        full[me[0], me[1]] = moment.astype(bf16)
        copies.append(send(
            1, lambda other: full.at[me[0], me[1]], lambda j: full.at[me[0], me[1]]
        ))

    again = []
    for (layer, _, _), sent in zip(layers, copies):
        full = layer["full"]
        finish(sent)
        again.append(send(0, lambda other: full.at[me[0]], lambda j: full.at[me[0]]))
    targets = ((w2_ref, new2_ref), (w3_ref, new3_ref))
    for (layer, _, _), sent, (w_ref, new_ref) in zip(layers, again, targets):
        full = layer["full"]
        finish(sent)
        rows = full.shape[2]
        for i in range(sizes[0]):
            for j in range(sizes[1]):
                at = (i * sizes[1] + j) * rows
                new_ref[at : at + rows, :] = w_ref[at : at + rows, :] - full[i, j].astype(f32)


def local(act_one, pre_two, cot_three, weight_two, weight_three, moment_two, moment_three):
    chan_one, chan_two, chan_three = (act_one.shape[1], pre_two.shape[1], cot_three.shape[1])
    local_d, local_h, local_w = pre_two.shape[2:]
    half_w = local_w // 2
    sizes = tuple(lax.axis_size(name) for name in AXES)
    scale_two = (chan_one * 27) ** (-0.5)
    scale_three = (chan_two * 27) ** (-0.5)
    bf16, f32 = (jnp.bfloat16, jnp.float32)

    def by_layer(x):
        return x[0].reshape(x.shape[1], x.shape[2], -1).transpose(1, 0, 2)

    act, cot, pre = (by_layer(act_one), by_layer(cot_three), by_layer(pre_two))
    layers3, lanes3 = (cot.shape[0] + 4, cot.shape[2] + 4 * half_w)
    layers2, lanes2 = (pre.shape[0] + 2, pre.shape[2] + 2 * local_w)
    inner3 = lanes3 - 2 * half_w
    held, blocks, moments = ([], [], [])
    for weight, moment in ((weight_two, moment_two), (weight_three, moment_three)):
        rows, width = (weight.shape[0] // (sizes[0] * sizes[1]), weight.shape[1])
        line = min(width, moment.shape[0])
        moments.append(moment.reshape(-1, line))
        blocks.append(jax.ShapeDtypeStruct((rows, width), f32))
        held += [
            pltpu.VMEM((sizes[0], sizes[1], rows, width), bf16),
            pltpu.VMEM((sizes[0] - 1, sizes[1], rows, width), bf16),
            pltpu.VMEM((sizes[1], rows, width), bf16),
            pltpu.VMEM((sizes[1] - 1, rows, width), bf16),
            pltpu.VMEM((rows, width), bf16),
            pltpu.VMEM((sizes[2], rows, width), bf16),
            pltpu.VMEM((sizes[2],) + moments[-1].shape, f32),
            pltpu.VMEM((sizes[0], sizes[1], rows, width), bf16),
        ]
    copies = 16 + 4 * (sum(sizes) - 3) + 2 * (sizes[2] - 1) + sizes[0] * sizes[1] - 1
    vmem = pl.BlockSpec(memory_space=pltpu.VMEM)
    grad_input, new_weight_two, new_weight_three, block_two, block_three = pl.pallas_call(
        functools.partial(
            step_kernel, half_w, (scale_two, scale_three),
            (scale_two / sizes[0], scale_three / sizes[0]),
        ),
        out_shape=(
            jax.ShapeDtypeStruct(act.shape, bf16),
            jax.ShapeDtypeStruct(weight_two.shape, f32),
            jax.ShapeDtypeStruct(weight_three.shape, f32),
            *blocks,
        ),
        in_specs=[vmem] * 7,
        out_specs=(vmem,) * 5,
        scratch_shapes=[
            pltpu.VMEM((layers3, chan_three, lanes3), bf16),
            pltpu.VMEM((layers2, chan_two, lanes2), bf16),
            pltpu.VMEM((9, 3 * chan_two, 27 * chan_two), bf16),
            pltpu.VMEM((9, 3 * chan_one, 27 * chan_one), bf16),
            pltpu.VMEM((layers3, 9 * chan_three, inner3), bf16),
            pltpu.VMEM((layers2, 3 * chan_two, lanes2), bf16),
            pltpu.VMEM((3 * chan_two, 9 * chan_three), bf16),
            pltpu.VMEM((9 * chan_one, 3 * chan_two), bf16),
            pltpu.VMEM((layers3 + 2, chan_two, inner3), f32),
            pltpu.VMEM((layers3 - 2, chan_two, 2 * inner3), f32),
            pltpu.VMEM((local_d, 3 * chan_one, lanes2), bf16),
            pltpu.VMEM((local_d // 2 + 2, 3 * chan_two, inner3), bf16),
            pltpu.VMEM((layers2 + 2, chan_one, act.shape[2]), f32),
            pltpu.VMEM(weight_two.shape, f32),
            pltpu.VMEM(weight_three.shape, f32),
            pltpu.VMEM((sizes[0] * sizes[1], 8, 128), f32),
            *held,
            pltpu.SemaphoreType.DMA((copies,)),
            pltpu.SemaphoreType.DMA((copies,)),
            pltpu.SemaphoreType.DMA((2,)),
        ],
        compiler_params=pltpu.CompilerParams(
            collective_id=0, has_side_effects=True, vmem_limit_bytes=56 * 2**20
        ),
        name="step",
    )(cot, pre, act, weight_two, weight_three, *moments)
    grad_input = grad_input.transpose(1, 0, 2).reshape(act_one.shape)
    mine = lax.axis_index("height")
    new_moment_two, new_moment_three = (
        lax.dynamic_slice_in_dim(block.reshape(-1), mine * moment.shape[0], moment.shape[0])
        for block, moment in ((block_two, moment_two), (block_three, moment_three))
    )
    return (grad_input, new_weight_two, new_weight_three, new_moment_two, new_moment_three)


def solution(mesh):
    in_specs = (
        P("dp", None, "depth", "height", None),
        P("dp", None, "depth", "height", None),
        P("dp", None, "depth", "height"),
        P(),
        P(),
        P(("dp", "depth", "height")),
        P(("dp", "depth", "height")),
    )
    out_specs = (
        P("dp", None, "depth", "height", None),
        P(),
        P(),
        P(("dp", "depth", "height")),
        P(("dp", "depth", "height")),
    )
    return jax.shard_map(local, mesh=mesh, in_specs=in_specs, out_specs=out_specs, check_vma=False)
```

```python
import functools

import jax
import jax.numpy as jnp
from jax import lax
from jax.experimental import pallas as pl
from jax.experimental.pallas import tpu as pltpu
from jax.sharding import PartitionSpec as P

AXES = ("dp", "depth", "height")
MESH = pl.DeviceIdType.MESH

SLOPE = 0.3
LEARN = 4.0
TRUST = 0.05
MOMENTUM = 0.9
EPSILON = 1e-06


def leaky(value):
    return jnp.where(value > 0, value, SLOPE * value)


def slope_of(value):
    return jnp.where(value > 0, 1.0, SLOPE).astype(jnp.float32)


def dot(a, b):
    return jnp.dot(a, b, preferred_element_type=jnp.float32)


def in_rows(ref, layer):
    rows = [ref[layer, r].astype(jnp.float32) for r in range(ref.shape[1])]
    return jnp.concatenate(rows, axis=1)


def dot_t(a, b):
    return lax.dot_general(a, b, (((1,), (1,)), ((), ())), preferred_element_type=jnp.float32)


def step_kernel(
    half_w, scales, rates, cot_ref, pre_ref, act_ref, w2_ref, w3_ref, m2_ref, m3_ref,
    gin_ref, new2_ref, new3_ref, mom2_ref, mom3_ref,
    cot_x, pre_x, perm3, perm2, wide3, wide2, taps3, taps2, back_acc, upper, act_wide, pool_wide,
    into, g2_acc, g3_acc, *rest,
):
    layer_refs, (send_sem, recv_sem, own_sem) = (rest[:-3], rest[-3:])
    per_layer = len(layer_refs) // 2
    names = ("parts", "arrived", "partial", "partials", "moments", "decayed", "full")
    layer2 = dict(zip(names, layer_refs[:per_layer]))
    layer3 = dict(zip(names, layer_refs[per_layer:]))
    me = [lax.axis_index(name) for name in AXES]
    sizes = [lax.axis_size(name) for name in AXES]
    last = [size - 1 for size in sizes]
    used = [0]

    def device(axis, index):
        return tuple(index if i == axis else me[i] for i in range(3))

    def others(axis):
        return [lax.rem(me[axis] + step, sizes[axis]) for step in range(1, sizes[axis])]

    def remote(source, target, to):
        n = used[0]
        used[0] += 1
        return pltpu.make_async_remote_copy(
            src_ref=source, dst_ref=target, send_sem=send_sem.at[n], recv_sem=recv_sem.at[n],
            device_id=to, device_id_type=MESH,
        )

    def send(axis, source, target):
        copies = []
        for j, other in enumerate(others(axis)):
            copy = remote(source(other), target(j), device(axis, other))
            copy.start()
            copies.append(copy)
        return copies

    peers = [
        (lax.rem(me[0] + i, sizes[0]), lax.rem(me[1] + j, sizes[1]))
        for i in range(sizes[0]) for j in range(sizes[1]) if i or j
    ]

    def send_all(source, target):
        copies = []
        for n, (a, b) in enumerate(peers):
            copy = remote(source(a, b), target(n), (a, b, me[2]))
            copy.start()
            copies.append(copy)
        return copies

    def finish(copies):
        for copy in copies:
            copy.wait()

    sides = [(d, h) for d in (-1, 0, 1) for h in (-1, 0, 1) if (d, h) != (0, 0)]

    def present(d, h):
        down, along = (me[1] + d, me[2] + h)
        return (down >= 0) & (down <= last[1]) & (along >= 0) & (along <= last[2])

    def part(side, length, width, taken):
        if side == 0:
            return pl.ds(0 if taken else width, length)
        if taken:
            return pl.ds(length - width if side > 0 else 0, width)
        return pl.ds(0 if side > 0 else width + length, width)

    arrays = ((cot_ref, cot_x, (2, 2 * half_w)), (pre_ref, pre_x, (1, 1)))

    def place(ref, width, d, h, taken):
        layers, along = (ref.shape[0], ref.shape[1 if ref.ndim == 4 else 2])
        where = (part(d, layers, width[0], taken), part(h, along, width[1], taken))
        return where if ref.ndim == 4 else (where[0], slice(None), where[1])

    barrier = pltpu.get_barrier_semaphore()

    def greet(to):
        pl.semaphore_signal(barrier, inc=1, device_id=to, device_id_type=MESH)

    for a, b in peers:
        greet((a, b, me[2]))
    for other in others(2):
        greet(device(2, other))
    for d, h in sides:
        if d and h:
            @pl.when(present(d, h))
            def _():
                greet((me[0], me[1] + d, me[2] + h))
    around = [jnp.where(me[i] > 0, 1, 0) + jnp.where(me[i] < last[i], 1, 0) for i in (1, 2)]
    pl.semaphore_wait(barrier, sizes[0] * sizes[1] + sizes[2] - 2 + around[0] * around[1])

    edges = [[], []]
    for a, (ref, out, width) in enumerate(arrays):
        for d, h in sides:
            copy = remote(
                ref.at[place(ref, width, d, h, True)], out.at[place(ref, width, d, h, False)],
                (me[0], me[1] + d, me[2] + h),
            )
            edges[a].append((d, h, copy))

            @pl.when(present(d, h))
            def _():
                copy.start()

    own = []
    for a, (ref, out, width) in enumerate(arrays):
        copy = pltpu.make_async_copy(ref, out.at[place(ref, width, 0, 0, False)], own_sem.at[a])
        copy.start()
        own.append(copy)
    moment_copies = []
    for layer, ref in ((layer2, m2_ref), (layer3, m3_ref)):
        layer["moments"][me[2]] = ref[...]
        moment_copies += send(
            2, lambda other: ref, lambda j: layer["moments"].at[me[2]]
        )
    for d, h in sides:
        @pl.when(jnp.logical_not(present(-d, -h)))
        def _():
            for ref, out, width in arrays:
                where = place(ref, width, d, h, False)
                if ref.ndim == 4:
                    shape = (where[0].size, where[1].size) + ref.shape[2:]
                else:
                    shape = (where[0].size, ref.shape[1], where[2].size)
                out[where] = jnp.zeros(shape, out.dtype)

    def finish_edges(a):
        own[a].wait()
        for d, h, copy in edges[a]:
            @pl.when(present(d, h))
            def _():
                copy.wait_send()

            @pl.when(present(-d, -h))
            def _():
                copy.wait_recv()

    bf16, f32 = (jnp.bfloat16, jnp.float32)
    chan_three, chan_two, chan_one = (cot_x.shape[1], pre_x.shape[2], act_ref.shape[2])
    wide = 2 * half_w
    layers3, lanes3 = (cot_x.shape[0], cot_x.shape[2])
    inner3 = lanes3 - wide
    layers2, lanes2 = (pre_x.shape[0], wide2.shape[2])
    own_layers, own_rows = act_ref.shape[:2]
    own_lanes = own_rows * wide
    rows2 = lanes2 // wide
    iota = lambda shape, dim: lax.broadcasted_iota(jnp.int32, shape, dim)
    depth, height = (me[1], me[2])
    one = lambda flag: jnp.where(flag, 1.0, 0.0).astype(f32)
    above, below = (one(depth > 0), one(depth < sizes[1] - 1))
    left, right = (one(height > 0), one(height < sizes[2] - 1))

    n3, n2 = (3 * chan_two, 3 * chan_one)
    row3, col3 = (iota((n3, 1), 0), iota((1, 27 * chan_two), 1))
    row2, col2 = (iota((n2, 1), 0), iota((1, 27 * chan_one), 1))
    for t in range(9):
        aim = (row3 % chan_two) * 27 + (row3 // chan_two) * 9 + t
        perm3[t] = jnp.where(col3 == aim, 1.0, 0.0).astype(bf16)
        aim = (row2 % chan_one) * 27 + (t // 3) * 9 + (row2 // chan_one) * 3 + t % 3
        perm2[t] = jnp.where(col2 == aim, 1.0, 0.0).astype(bf16)
    w3, w2 = (w3_ref[...].astype(bf16), w2_ref[...].astype(bf16))
    for t in range(9):
        taps3[:, t * chan_three : (t + 1) * chan_three] = dot(perm3[t], w3).astype(bf16)
    for kd in range(3):
        taps2[kd * n2 : (kd + 1) * n2, :] = jnp.concatenate(
            [dot_t(perm2[kd * 3 + kw], w2) for kw in range(3)], axis=1
        ).astype(bf16)

    norms = [
        jnp.sqrt(jnp.sum(jnp.sum(w * w, axis=0, keepdims=True), axis=1, keepdims=True))
        for w in (w2_ref[...], w3_ref[...])
    ]
    halves = jnp.where(iota((2 * wide, wide), 0) // 2 == iota((2 * wide, wide), 1), 0.125, 0.0)
    halves = halves.astype(bf16)
    coarse = own_layers // 2
    pool_wide[...] = jnp.zeros_like(pool_wide)
    for d in range(coarse):
        total = leaky(in_rows(pre_ref, 2 * d)) + leaky(in_rows(pre_ref, 2 * d + 1))
        coarse_rows = inner3 // half_w
        sums = []
        for q in range(coarse_rows):
            if q in (0, coarse_rows - 1):
                sums.append(jnp.zeros((chan_two, wide), f32))
            else:
                at = (2 * q - 2) * wide
                sums.append(total[:, at : at + wide] + total[:, at + wide : at + 2 * wide])
        for pair in range(coarse_rows // 2):
            both = jnp.concatenate(sums[2 * pair : 2 * pair + 2], axis=1)
            high = both.astype(bf16)
            low = (both - high.astype(f32)).astype(bf16)
            mean = (dot(high, halves) + dot(low, halves)).astype(bf16)
            for kd in range(3):
                pool_wide[
                    d + 2 - kd, kd * chan_two : (kd + 1) * chan_two, pair * wide : (pair + 1) * wide
                ] = mean

    def old_moment(layer, width):
        pieces = [layer["moments"][c] for c in range(sizes[2])]
        split = width // pieces[0].shape[1]
        lines = [
            pieces[c] if split == 1 else jnp.concatenate(pieces[c : c + split], axis=1)
            for c in range(0, sizes[2], split)
        ]
        return lines[0] if len(lines) == 1 else jnp.concatenate(lines, axis=0)

    finish(moment_copies)
    decayed_copies = []
    for layer in (layer2, layer3):
        decayed = layer["decayed"].at[me[0], me[1]]
        old = old_moment(layer, layer["decayed"].shape[3])
        decayed[...] = (MOMENTUM * old).astype(bf16)
        decayed_copies += send_all(lambda a, b: decayed, lambda n: decayed)
    finish_edges(0)

    back_acc[...] = jnp.zeros_like(back_acc)
    column3 = iota((1, lanes3), 1) % half_w

    @pl.loop(0, layers3)
    def _(e):
        whole = cot_x[e].astype(f32)
        for kw in range(3):
            ow = 2 - kw
            moved = whole
            if ow == 0:
                moved = jnp.where(column3 == 0, 0.0, pltpu.roll(whole, 1, 1))
            elif ow == 2:
                moved = jnp.where(column3 == half_w - 1, 0.0, pltpu.roll(whole, lanes3 - 1, 1))
            for kh in range(3):
                start = (2 - kh) * half_w
                piece = moved if start == 0 else pltpu.roll(moved, lanes3 - start, 1)
                t = kh * 3 + kw
                wide3[e, t * chan_three : (t + 1) * chan_three, :] = piece[:, :inner3].astype(bf16)
        product = dot(taps3[...], wide3[e])
        for kd in range(3):
            back_acc[e + kd] += product[kd * chan_two : (kd + 1) * chan_two]

    twice = jnp.where(iota((wide, 2 * wide), 0) == iota((wide, 2 * wide), 1) // 2, 1.0, 0.0)
    twice = twice.astype(bf16)
    for layer in range(layers3 - 2):
        cells = (scales[1] * back_acc[layer + 2]).astype(bf16)
        for pair in range(inner3 // wide):
            upper[layer, :, pair * 2 * wide : (pair + 1) * 2 * wide] = dot(
                cells[:, pair * wide : (pair + 1) * wide], twice
            )

    for t in range(9):
        rows = slice(t * chan_three, (t + 1) * chan_three)
        grad = dot_t(wide3[1, rows, :], pool_wide[0])
        for e in range(1, coarse + 2):
            grad = grad + dot_t(wide3[e + 1, rows, :], pool_wide[e])
        ordered = dot(grad.astype(bf16), perm3[t])
        if t == 0:
            g3_acc[...] = ordered
        else:
            g3_acc[...] += ordered

    def first_sum(layer, acc):
        parts, arrived = (layer["parts"], layer["arrived"])
        rows = parts.shape[2]
        for i in range(sizes[0]):
            for j in range(sizes[1]):
                at = (i * sizes[1] + j) * rows
                parts[i, j] = acc[at : at + rows].astype(bf16)
        return send_all(lambda a, b: parts.at[a, b], lambda n: arrived.at[n])

    def second_sum(layer, copies):
        finish(copies)
        total = layer["parts"][me[0], me[1]].astype(f32)
        for n in range(len(peers)):
            total = total + layer["arrived"][n].astype(f32)
        layer["partial"][...] = total.astype(bf16)
        layer["partials"][me[2]] = layer["partial"][...]
        return send(2, lambda other: layer["partial"], lambda j: layer["partials"].at[me[2]])

    def gather(layer, copies, rate, mom_ref):
        finish(copies)
        total = layer["partials"][0].astype(f32)
        for j in range(1, sizes[2]):
            total = total + layer["partials"][j].astype(f32)
        mom_ref[...] = total * rate
        mine = layer["full"].at[me[0], me[1]]
        mine[...] = mom_ref[...].astype(bf16)
        return send_all(lambda a, b: mine, lambda n: mine)

    copies3 = first_sum(layer3, g3_acc)
    finish_edges(1)

    column2 = iota((1, lanes2), 1) % wide
    lane = iota((1, lanes2), 1)
    edge = jnp.where(lane < wide, left, jnp.where(lane >= lanes2 - wide, right, 1.0))
    into[...] = jnp.zeros_like(into)

    @pl.loop(0, layers2)
    def _(f):
        parent = upper[(f + 1) // 2]
        cells = [parent[:, (r + 1) // 2 * wide : ((r + 1) // 2 + 1) * wide] for r in range(rows2)]
        spread = jnp.concatenate(cells, axis=1)
        inside = edge * jnp.where(f == 0, above, jnp.where(f == layers2 - 1, below, 1.0))
        value = spread * 0.125 * slope_of(in_rows(pre_x, f))
        value = jnp.where(inside > 0, value, 0.0)
        before = jnp.where(column2 == 0, 0.0, pltpu.roll(value, 1, 1))
        after = jnp.where(column2 == wide - 1, 0.0, pltpu.roll(value, lanes2 - 1, 1))
        for kw, moved in enumerate((after, value, before)):
            wide2[f, kw * chan_two : (kw + 1) * chan_two, :] = moved.astype(bf16)

    copies3 = second_sum(layer3, copies3)

    act_wide[...] = jnp.zeros_like(act_wide)
    for d in range(own_layers):
        for kh in range(3):
            start = (2 - kh) * wide
            for r in range(own_rows):
                at = start + r * wide
                act_wide[d, kh * chan_one : (kh + 1) * chan_one, at : at + wide] = act_ref[d, r]
    n_wide = 3 * chan_two
    for kd in range(3):
        grad = dot_t(wide2[2 - kd], act_wide[0])
        for d in range(1, own_layers):
            grad = grad + dot_t(wide2[d + 2 - kd], act_wide[d])
        grad = grad.astype(bf16)
        for kw in range(3):
            ordered = dot(grad[kw * chan_two : (kw + 1) * chan_two], perm2[kd * 3 + kw])
            if kd == 0 and kw == 0:
                g2_acc[...] = ordered
            else:
                g2_acc[...] += ordered

    copies2 = first_sum(layer2, g2_acc)
    full3 = gather(layer3, copies3, rates[1], mom3_ref)

    def input_step(f):
        product = dot(taps2[...], wide2[f])
        for kd in range(3):
            total = None
            for kh in range(3):
                at, start = ((kd * 3 + kh) * chan_one, (2 - kh) * wide)
                term = product[at : at + chan_one, start : start + own_lanes]
                total = term if total is None else total + term
            into[f + kd] += total

    third = layers2 // 3
    for f in range(third):
        input_step(f)
    copies2 = second_sum(layer2, copies2)
    for f in range(third, 2 * third):
        input_step(f)
    full2 = gather(layer2, copies2, rates[0], mom2_ref)
    for f in range(2 * third, layers2):
        input_step(f)
    for d in range(own_layers):
        value = (scales[0] * into[d + 2]).astype(bf16)
        for r in range(own_rows):
            gin_ref[d, r] = value[:, r * wide : (r + 1) * wide]

    finish(decayed_copies)
    steps = []
    for n, (layer, copies, mom_ref) in enumerate(((layer2, full2, mom2_ref), (layer3, full3, mom3_ref))):
        finish(copies)
        full, decayed = (layer["full"], layer["decayed"])
        blocks = [(i, j) for i in range(sizes[0]) for j in range(sizes[1])]
        grad = jnp.concatenate([full[i, j].astype(f32) for i, j in blocks], axis=0)
        square = jnp.sum(jnp.sum(grad * grad, axis=0, keepdims=True), axis=1, keepdims=True)
        rate = LEARN * TRUST * norms[n] / (jnp.sqrt(square) + EPSILON)
        mom_ref[...] = MOMENTUM * old_moment(layer, mom_ref.shape[1]) + rate * mom_ref[...]
        held = jnp.concatenate([decayed[i, j].astype(f32) for i, j in blocks], axis=0)
        steps.append(held + rate * grad)
    new2_ref[...] = w2_ref[...] - steps[0]
    width = steps[1].shape[1]
    for at in range(0, width, 128):
        end = min(at + 128, width)
        new3_ref[at:end, :] = w3_ref[at:end, :] - steps[1][:, at:end].T


def local(act_one, pre_two, cot_three, weight_two, weight_three, moment_two, moment_three):
    chan_one, chan_two, chan_three = (act_one.shape[1], pre_two.shape[1], cot_three.shape[1])
    local_d, local_h, local_w = pre_two.shape[2:]
    half_w = local_w // 2
    sizes = tuple(lax.axis_size(name) for name in AXES)
    scale_two = (chan_one * 27) ** (-0.5)
    scale_three = (chan_two * 27) ** (-0.5)
    bf16, f32 = (jnp.bfloat16, jnp.float32)

    def by_layer(x):
        return x[0].reshape(x.shape[1], x.shape[2], -1).transpose(1, 0, 2)

    def by_row(x):
        rows = x[0].reshape(x.shape[1], -1, x.shape[4]).transpose(1, 0, 2)
        return rows.reshape(x.shape[2], x.shape[3], x.shape[1], x.shape[4])

    act, cot, pre = (by_row(act_one), by_layer(cot_three), by_row(pre_two))
    layers3, lanes3 = (cot.shape[0] + 4, cot.shape[2] + 4 * half_w)
    layers2, lanes2 = (pre.shape[0] + 2, (pre.shape[1] + 2) * local_w)
    inner3 = lanes3 - 2 * half_w
    held, blocks, moments = ([], [], [])
    for weight, moment in ((weight_two, moment_two), (weight_three, moment_three)):
        rows, width = (weight.shape[0] // (sizes[0] * sizes[1]), weight.shape[1])
        line = min(width, moment.shape[0])
        moments.append(moment.reshape(-1, line))
        blocks.append(jax.ShapeDtypeStruct((rows, width), f32))
        held += [
            pltpu.VMEM((sizes[0], sizes[1], rows, width), bf16),
            pltpu.VMEM((sizes[0] * sizes[1] - 1, rows, width), bf16),
            pltpu.VMEM((rows, width), bf16),
            pltpu.VMEM((sizes[2], rows, width), bf16),
            pltpu.VMEM((sizes[2],) + moments[-1].shape, f32),
            pltpu.VMEM((sizes[0], sizes[1], rows, width), bf16),
            pltpu.VMEM((sizes[0], sizes[1], rows, width), bf16),
        ]
    copies = 16 + 4 * (sizes[2] - 1) + 6 * (sizes[0] * sizes[1] - 1)
    vmem = pl.BlockSpec(memory_space=pltpu.VMEM)
    grad_input, new_weight_two, new_weight_three, block_two, block_three = pl.pallas_call(
        functools.partial(
            step_kernel, half_w, (scale_two, scale_three),
            (scale_two / sizes[0], scale_three / sizes[0]),
        ),
        out_shape=(
            jax.ShapeDtypeStruct(act.shape, bf16),
            jax.ShapeDtypeStruct(weight_two.shape, f32),
            jax.ShapeDtypeStruct(weight_three.shape[::-1], f32),
            *blocks,
        ),
        in_specs=[vmem] * 7,
        out_specs=(vmem,) * 5,
        scratch_shapes=[
            pltpu.VMEM((layers3, chan_three, lanes3), bf16),
            pltpu.VMEM((layers2, lanes2 // local_w, chan_two, local_w), bf16),
            pltpu.VMEM((9, 3 * chan_two, 27 * chan_two), bf16),
            pltpu.VMEM((9, 3 * chan_one, 27 * chan_one), bf16),
            pltpu.VMEM((layers3, 9 * chan_three, inner3), bf16),
            pltpu.VMEM((layers2, 3 * chan_two, lanes2), bf16),
            pltpu.VMEM((3 * chan_two, 9 * chan_three), bf16),
            pltpu.VMEM((9 * chan_one, 3 * chan_two), bf16),
            pltpu.VMEM((layers3 + 2, chan_two, inner3), f32),
            pltpu.VMEM((layers3 - 2, chan_two, 2 * inner3), f32),
            pltpu.VMEM((local_d, 3 * chan_one, lanes2), bf16),
            pltpu.VMEM((local_d // 2 + 2, 3 * chan_two, inner3), bf16),
            pltpu.VMEM((layers2 + 2, chan_one, local_h * local_w), f32),
            pltpu.VMEM(weight_two.shape, f32),
            pltpu.VMEM(weight_three.shape, f32),
            *held,
            pltpu.SemaphoreType.DMA((copies,)),
            pltpu.SemaphoreType.DMA((copies,)),
            pltpu.SemaphoreType.DMA((2,)),
        ],
        compiler_params=pltpu.CompilerParams(
            collective_id=0, has_side_effects=True, vmem_limit_bytes=56 * 2**20
        ),
        name="step",
    )(cot, pre, act, weight_two, weight_three.T, *moments)
    grad_input = grad_input.transpose(2, 0, 1, 3)[None]
    new_weight_three = new_weight_three.T
    mine = lax.axis_index("height")
    new_moment_two, new_moment_three = (
        lax.dynamic_slice_in_dim(block.reshape(-1), mine * moment.shape[0], moment.shape[0])
        for block, moment in ((block_two, moment_two), (block_three, moment_three))
    )
    return (grad_input, new_weight_two, new_weight_three, new_moment_two, new_moment_three)


def solution(mesh):
    in_specs = (
        P("dp", None, "depth", "height", None),
        P("dp", None, "depth", "height", None),
        P("dp", None, "depth", "height"),
        P(),
        P(),
        P(("dp", "depth", "height")),
        P(("dp", "depth", "height")),
    )
    out_specs = (
        P("dp", None, "depth", "height", None),
        P(),
        P(),
        P(("dp", "depth", "height")),
        P(("dp", "depth", "height")),
    )
    return jax.shard_map(local, mesh=mesh, in_specs=in_specs, out_specs=out_specs, check_vma=False)
```

```python
import functools

import jax
import jax.numpy as jnp
from jax import lax
from jax.experimental import pallas as pl
from jax.experimental.pallas import tpu as pltpu
from jax.sharding import PartitionSpec as P

AXES = ("dp", "depth", "height")
MESH = pl.DeviceIdType.MESH

SLOPE = 0.3
LEARN = 4.0
TRUST = 0.05
MOMENTUM = 0.9
EPSILON = 1e-06


def leaky(value):
    return jnp.where(value > 0, value, SLOPE * value)


def slope_of(value):
    return jnp.where(value > 0, 1.0, SLOPE).astype(jnp.float32)


def dot(a, b):
    return jnp.dot(a, b, preferred_element_type=jnp.float32)


def in_rows(ref, layer):
    rows = [ref[layer, r].astype(jnp.float32) for r in range(ref.shape[1])]
    return jnp.concatenate(rows, axis=1)


def dot_t(a, b):
    return lax.dot_general(a, b, (((1,), (1,)), ((), ())), preferred_element_type=jnp.float32)


def step_kernel(
    half_w, scales, rates, cot_ref, pre_ref, act_ref, w2_ref, w3_ref, m2_ref, m3_ref,
    gin_ref, new2_ref, new3_ref, mom2_ref, mom3_ref,
    cot_x, pre_x, perm3, perm2, wide3, wide2, taps3, taps2, back_acc, upper, act_wide, pool_wide,
    into, g2_acc, g3_acc, *rest,
):
    layer_refs, (send_sem, recv_sem, own_sem) = (rest[:-3], rest[-3:])
    per_layer = len(layer_refs) // 2
    names = ("parts", "arrived", "partial", "partials", "moments", "decayed", "full")
    layer2 = dict(zip(names, layer_refs[:per_layer]))
    layer3 = dict(zip(names, layer_refs[per_layer:]))
    me = [lax.axis_index(name) for name in AXES]
    sizes = [lax.axis_size(name) for name in AXES]
    last = [size - 1 for size in sizes]
    used = [0]

    def device(axis, index):
        return tuple(index if i == axis else me[i] for i in range(3))

    def others(axis):
        return [lax.rem(me[axis] + step, sizes[axis]) for step in range(1, sizes[axis])]

    def remote(source, target, to):
        n = used[0]
        used[0] += 1
        return pltpu.make_async_remote_copy(
            src_ref=source, dst_ref=target, send_sem=send_sem.at[n], recv_sem=recv_sem.at[n],
            device_id=to, device_id_type=MESH,
        )

    def send(axis, source, target):
        copies = []
        for j, other in enumerate(others(axis)):
            copy = remote(source(other), target(j), device(axis, other))
            copy.start()
            copies.append(copy)
        return copies

    peers = [
        (lax.rem(me[0] + i, sizes[0]), lax.rem(me[1] + j, sizes[1]))
        for i in range(sizes[0]) for j in range(sizes[1]) if i or j
    ]

    def send_all(source, target):
        copies = []
        for n, (a, b) in enumerate(peers):
            copy = remote(source(a, b), target(n), (a, b, me[2]))
            copy.start()
            copies.append(copy)
        return copies

    def finish(copies):
        for copy in copies:
            copy.wait()

    sides = [(d, h) for d in (-1, 0, 1) for h in (-1, 0, 1) if (d, h) != (0, 0)]

    def present(d, h):
        down, along = (me[1] + d, me[2] + h)
        return (down >= 0) & (down <= last[1]) & (along >= 0) & (along <= last[2])

    def part(side, length, width, taken):
        if side == 0:
            return pl.ds(0 if taken else width, length)
        if taken:
            return pl.ds(length - width if side > 0 else 0, width)
        return pl.ds(0 if side > 0 else width + length, width)

    arrays = ((cot_ref, cot_x, (2, 2 * half_w)), (pre_ref, pre_x, (1, 1)))

    def place(ref, width, d, h, taken):
        layers, along = (ref.shape[0], ref.shape[1 if ref.ndim == 4 else 2])
        where = (part(d, layers, width[0], taken), part(h, along, width[1], taken))
        return where if ref.ndim == 4 else (where[0], slice(None), where[1])

    barrier = pltpu.get_barrier_semaphore()

    def greet(to):
        pl.semaphore_signal(barrier, inc=1, device_id=to, device_id_type=MESH)

    for a, b in peers:
        greet((a, b, me[2]))
    for other in others(2):
        greet(device(2, other))
    for d, h in sides:
        if d and h:
            @pl.when(present(d, h))
            def _():
                greet((me[0], me[1] + d, me[2] + h))
    around = [jnp.where(me[i] > 0, 1, 0) + jnp.where(me[i] < last[i], 1, 0) for i in (1, 2)]
    pl.semaphore_wait(barrier, sizes[0] * sizes[1] + sizes[2] - 2 + around[0] * around[1])

    edges = [[], []]
    for a, (ref, out, width) in enumerate(arrays):
        for d, h in sides:
            copy = remote(
                ref.at[place(ref, width, d, h, True)], out.at[place(ref, width, d, h, False)],
                (me[0], me[1] + d, me[2] + h),
            )
            edges[a].append((d, h, copy))

    def start_edges(a):
        for d, h, copy in edges[a]:
            @pl.when(present(d, h))
            def _():
                copy.start()

    start_edges(0)
    own = []
    for a, (ref, out, width) in enumerate(arrays):
        copy = pltpu.make_async_copy(ref, out.at[place(ref, width, 0, 0, False)], own_sem.at[a])
        copy.start()
        own.append(copy)
    moment_copies = []
    for layer, ref in ((layer2, m2_ref), (layer3, m3_ref)):
        layer["moments"][me[2]] = ref[...]
        moment_copies += send(
            2, lambda other: ref, lambda j: layer["moments"].at[me[2]]
        )
    for d, h in sides:
        @pl.when(jnp.logical_not(present(-d, -h)))
        def _():
            for ref, out, width in arrays:
                where = place(ref, width, d, h, False)
                if ref.ndim == 4:
                    shape = (where[0].size, where[1].size) + ref.shape[2:]
                else:
                    shape = (where[0].size, ref.shape[1], where[2].size)
                out[where] = jnp.zeros(shape, out.dtype)

    def finish_edges(a):
        own[a].wait()
        for d, h, copy in edges[a]:
            @pl.when(present(d, h))
            def _():
                copy.wait_send()

            @pl.when(present(-d, -h))
            def _():
                copy.wait_recv()

    bf16, f32 = (jnp.bfloat16, jnp.float32)
    chan_three, chan_two, chan_one = (cot_x.shape[1], pre_x.shape[2], act_ref.shape[2])
    wide = 2 * half_w
    layers3, lanes3 = (cot_x.shape[0], cot_x.shape[2])
    inner3 = lanes3 - wide
    layers2, lanes2 = (pre_x.shape[0], wide2.shape[2])
    own_layers, own_rows = act_ref.shape[:2]
    own_lanes = own_rows * wide
    rows2 = lanes2 // wide
    iota = lambda shape, dim: lax.broadcasted_iota(jnp.int32, shape, dim)
    depth, height = (me[1], me[2])
    one = lambda flag: jnp.where(flag, 1.0, 0.0).astype(f32)
    above, below = (one(depth > 0), one(depth < sizes[1] - 1))
    left, right = (one(height > 0), one(height < sizes[2] - 1))

    n3, n2 = (3 * chan_two, 3 * chan_one)
    row3, col3 = (iota((n3, 1), 0), iota((1, 27 * chan_two), 1))
    row2, col2 = (iota((n2, 1), 0), iota((1, 27 * chan_one), 1))
    for t in range(9):
        aim = (row3 % chan_two) * 27 + (row3 // chan_two) * 9 + t
        perm3[t] = jnp.where(col3 == aim, 1.0, 0.0).astype(bf16)
        aim = (row2 % chan_one) * 27 + (t // 3) * 9 + (row2 // chan_one) * 3 + t % 3
        perm2[t] = jnp.where(col2 == aim, 1.0, 0.0).astype(bf16)
    w3, w2 = (w3_ref[...].astype(bf16), w2_ref[...].astype(bf16))
    for t in range(9):
        taps3[:, t * chan_three : (t + 1) * chan_three] = dot(perm3[t], w3).astype(bf16)
    for kd in range(3):
        taps2[kd * n2 : (kd + 1) * n2, :] = jnp.concatenate(
            [dot_t(perm2[kd * 3 + kw], w2) for kw in range(3)], axis=1
        ).astype(bf16)

    norms = [
        jnp.sqrt(jnp.sum(jnp.sum(w * w, axis=0, keepdims=True), axis=1, keepdims=True))
        for w in (w2_ref[...], w3_ref[...])
    ]
    halves = jnp.where(iota((2 * wide, wide), 0) // 2 == iota((2 * wide, wide), 1), 0.125, 0.0)
    halves = halves.astype(bf16)
    coarse = own_layers // 2
    pool_wide[...] = jnp.zeros_like(pool_wide)
    for d in range(coarse):
        total = leaky(in_rows(pre_ref, 2 * d)) + leaky(in_rows(pre_ref, 2 * d + 1))
        coarse_rows = inner3 // half_w
        sums = []
        for q in range(coarse_rows):
            if q in (0, coarse_rows - 1):
                sums.append(jnp.zeros((chan_two, wide), f32))
            else:
                at = (2 * q - 2) * wide
                sums.append(total[:, at : at + wide] + total[:, at + wide : at + 2 * wide])
        for pair in range(coarse_rows // 2):
            both = jnp.concatenate(sums[2 * pair : 2 * pair + 2], axis=1)
            high = both.astype(bf16)
            low = (both - high.astype(f32)).astype(bf16)
            mean = (dot(high, halves) + dot(low, halves)).astype(bf16)
            for kd in range(3):
                pool_wide[
                    d + 2 - kd, kd * chan_two : (kd + 1) * chan_two, pair * wide : (pair + 1) * wide
                ] = mean

    def old_moment(layer, width):
        pieces = [layer["moments"][c] for c in range(sizes[2])]
        split = width // pieces[0].shape[1]
        lines = [
            pieces[c] if split == 1 else jnp.concatenate(pieces[c : c + split], axis=1)
            for c in range(0, sizes[2], split)
        ]
        return lines[0] if len(lines) == 1 else jnp.concatenate(lines, axis=0)

    finish_edges(0)
    start_edges(1)

    back_acc[...] = jnp.zeros_like(back_acc)
    column3 = iota((1, lanes3), 1) % half_w

    @pl.loop(0, layers3)
    def _(e):
        whole = cot_x[e].astype(f32)
        for kw in range(3):
            ow = 2 - kw
            moved = whole
            if ow == 0:
                moved = jnp.where(column3 == 0, 0.0, pltpu.roll(whole, 1, 1))
            elif ow == 2:
                moved = jnp.where(column3 == half_w - 1, 0.0, pltpu.roll(whole, lanes3 - 1, 1))
            for kh in range(3):
                start = (2 - kh) * half_w
                piece = moved if start == 0 else pltpu.roll(moved, lanes3 - start, 1)
                t = kh * 3 + kw
                wide3[e, t * chan_three : (t + 1) * chan_three, :] = piece[:, :inner3].astype(bf16)
        product = dot(taps3[...], wide3[e])
        for kd in range(3):
            back_acc[e + kd] += product[kd * chan_two : (kd + 1) * chan_two]

    twice = jnp.where(iota((wide, 2 * wide), 0) == iota((wide, 2 * wide), 1) // 2, 1.0, 0.0)
    twice = twice.astype(bf16)
    for layer in range(layers3 - 2):
        cells = (scales[1] * back_acc[layer + 2]).astype(bf16)
        for pair in range(inner3 // wide):
            upper[layer, :, pair * 2 * wide : (pair + 1) * 2 * wide] = dot(
                cells[:, pair * wide : (pair + 1) * wide], twice
            )

    for t in range(9):
        rows = slice(t * chan_three, (t + 1) * chan_three)
        grad = dot_t(wide3[1, rows, :], pool_wide[0])
        for e in range(1, coarse + 2):
            grad = grad + dot_t(wide3[e + 1, rows, :], pool_wide[e])
        ordered = dot(grad.astype(bf16), perm3[t])
        if t == 0:
            g3_acc[...] = ordered
        else:
            g3_acc[...] += ordered

    def first_sum(layer, acc):
        parts, arrived = (layer["parts"], layer["arrived"])
        rows = parts.shape[2]
        for i in range(sizes[0]):
            for j in range(sizes[1]):
                at = (i * sizes[1] + j) * rows
                parts[i, j] = acc[at : at + rows].astype(bf16)
        return send_all(lambda a, b: parts.at[a, b], lambda n: arrived.at[n])

    def second_sum(layer, copies):
        finish(copies)
        total = layer["parts"][me[0], me[1]].astype(f32)
        for n in range(len(peers)):
            total = total + layer["arrived"][n].astype(f32)
        layer["partial"][...] = total.astype(bf16)
        layer["partials"][me[2]] = layer["partial"][...]
        return send(2, lambda other: layer["partial"], lambda j: layer["partials"].at[me[2]])

    def gather(layer, copies, rate, mom_ref):
        finish(copies)
        total = layer["partials"][0].astype(f32)
        for j in range(1, sizes[2]):
            total = total + layer["partials"][j].astype(f32)
        mom_ref[...] = total * rate
        mine = layer["full"].at[me[0], me[1]]
        mine[...] = mom_ref[...].astype(bf16)
        return send_all(lambda a, b: mine, lambda n: mine)

    copies3 = first_sum(layer3, g3_acc)
    finish_edges(1)

    column2 = iota((1, lanes2), 1) % wide
    lane = iota((1, lanes2), 1)
    edge = jnp.where(lane < wide, left, jnp.where(lane >= lanes2 - wide, right, 1.0))
    into[...] = jnp.zeros_like(into)

    @pl.loop(0, layers2)
    def _(f):
        parent = upper[(f + 1) // 2]
        cells = [parent[:, (r + 1) // 2 * wide : ((r + 1) // 2 + 1) * wide] for r in range(rows2)]
        spread = jnp.concatenate(cells, axis=1)
        inside = edge * jnp.where(f == 0, above, jnp.where(f == layers2 - 1, below, 1.0))
        value = spread * 0.125 * slope_of(in_rows(pre_x, f))
        value = jnp.where(inside > 0, value, 0.0)
        before = jnp.where(column2 == 0, 0.0, pltpu.roll(value, 1, 1))
        after = jnp.where(column2 == wide - 1, 0.0, pltpu.roll(value, lanes2 - 1, 1))
        for kw, moved in enumerate((after, value, before)):
            wide2[f, kw * chan_two : (kw + 1) * chan_two, :] = moved.astype(bf16)

    copies3 = second_sum(layer3, copies3)
    finish(moment_copies)
    decayed_copies = []
    for layer in (layer2, layer3):
        decayed = layer["decayed"].at[me[0], me[1]]
        old = old_moment(layer, layer["decayed"].shape[3])
        decayed[...] = (MOMENTUM * old).astype(bf16)
        decayed_copies += send_all(lambda a, b: decayed, lambda n: decayed)

    act_wide[...] = jnp.zeros_like(act_wide)
    for d in range(own_layers):
        for kh in range(3):
            start = (2 - kh) * wide
            for r in range(own_rows):
                at = start + r * wide
                act_wide[d, kh * chan_one : (kh + 1) * chan_one, at : at + wide] = act_ref[d, r]
    n_wide = 3 * chan_two
    for kd in range(3):
        grad = dot_t(wide2[2 - kd], act_wide[0])
        for d in range(1, own_layers):
            grad = grad + dot_t(wide2[d + 2 - kd], act_wide[d])
        grad = grad.astype(bf16)
        for kw in range(3):
            ordered = dot(grad[kw * chan_two : (kw + 1) * chan_two], perm2[kd * 3 + kw])
            if kd == 0 and kw == 0:
                g2_acc[...] = ordered
            else:
                g2_acc[...] += ordered

    copies2 = first_sum(layer2, g2_acc)
    full3 = gather(layer3, copies3, rates[1], mom3_ref)

    def input_step(f):
        product = dot(taps2[...], wide2[f])
        for kd in range(3):
            total = None
            for kh in range(3):
                at, start = ((kd * 3 + kh) * chan_one, (2 - kh) * wide)
                term = product[at : at + chan_one, start : start + own_lanes]
                total = term if total is None else total + term
            into[f + kd] += total

    third = layers2 // 3
    for f in range(third):
        input_step(f)
    copies2 = second_sum(layer2, copies2)
    for f in range(third, 2 * third):
        input_step(f)
    full2 = gather(layer2, copies2, rates[0], mom2_ref)
    for f in range(2 * third, layers2):
        input_step(f)
    for d in range(own_layers):
        value = (scales[0] * into[d + 2]).astype(bf16)
        for r in range(own_rows):
            gin_ref[d, r] = value[:, r * wide : (r + 1) * wide]

    finish(decayed_copies)
    steps = []
    for n, (layer, copies, mom_ref) in enumerate(((layer2, full2, mom2_ref), (layer3, full3, mom3_ref))):
        finish(copies)
        full, decayed = (layer["full"], layer["decayed"])
        blocks = [(i, j) for i in range(sizes[0]) for j in range(sizes[1])]
        grad = jnp.concatenate([full[i, j].astype(f32) for i, j in blocks], axis=0)
        square = jnp.sum(jnp.sum(grad * grad, axis=0, keepdims=True), axis=1, keepdims=True)
        rate = LEARN * TRUST * norms[n] / (jnp.sqrt(square) + EPSILON)
        mom_ref[...] = MOMENTUM * old_moment(layer, mom_ref.shape[1]) + rate * mom_ref[...]
        held = jnp.concatenate([decayed[i, j].astype(f32) for i, j in blocks], axis=0)
        steps.append(held + rate * grad)
    new2_ref[...] = w2_ref[...] - steps[0]
    width = steps[1].shape[1]
    for at in range(0, width, 128):
        end = min(at + 128, width)
        new3_ref[at:end, :] = w3_ref[at:end, :] - steps[1][:, at:end].T


def local(act_one, pre_two, cot_three, weight_two, weight_three, moment_two, moment_three):
    chan_one, chan_two, chan_three = (act_one.shape[1], pre_two.shape[1], cot_three.shape[1])
    local_d, local_h, local_w = pre_two.shape[2:]
    half_w = local_w // 2
    sizes = tuple(lax.axis_size(name) for name in AXES)
    scale_two = (chan_one * 27) ** (-0.5)
    scale_three = (chan_two * 27) ** (-0.5)
    bf16, f32 = (jnp.bfloat16, jnp.float32)

    def by_layer(x):
        return x[0].reshape(x.shape[1], x.shape[2], -1).transpose(1, 0, 2)

    def by_row(x):
        rows = x[0].reshape(x.shape[1], -1, x.shape[4]).transpose(1, 0, 2)
        return rows.reshape(x.shape[2], x.shape[3], x.shape[1], x.shape[4])

    act, cot, pre = (by_row(act_one), by_layer(cot_three), by_row(pre_two))
    layers3, lanes3 = (cot.shape[0] + 4, cot.shape[2] + 4 * half_w)
    layers2, lanes2 = (pre.shape[0] + 2, (pre.shape[1] + 2) * local_w)
    inner3 = lanes3 - 2 * half_w
    held, blocks, moments = ([], [], [])
    for weight, moment in ((weight_two, moment_two), (weight_three, moment_three)):
        rows, width = (weight.shape[0] // (sizes[0] * sizes[1]), weight.shape[1])
        line = min(width, moment.shape[0])
        moments.append(moment.reshape(-1, line))
        blocks.append(jax.ShapeDtypeStruct((rows, width), f32))
        held += [
            pltpu.VMEM((sizes[0], sizes[1], rows, width), bf16),
            pltpu.VMEM((sizes[0] * sizes[1] - 1, rows, width), bf16),
            pltpu.VMEM((rows, width), bf16),
            pltpu.VMEM((sizes[2], rows, width), bf16),
            pltpu.VMEM((sizes[2],) + moments[-1].shape, f32),
            pltpu.VMEM((sizes[0], sizes[1], rows, width), bf16),
            pltpu.VMEM((sizes[0], sizes[1], rows, width), bf16),
        ]
    copies = 16 + 4 * (sizes[2] - 1) + 6 * (sizes[0] * sizes[1] - 1)
    vmem = pl.BlockSpec(memory_space=pltpu.VMEM)
    grad_input, new_weight_two, new_weight_three, block_two, block_three = pl.pallas_call(
        functools.partial(
            step_kernel, half_w, (scale_two, scale_three),
            (scale_two / sizes[0], scale_three / sizes[0]),
        ),
        out_shape=(
            jax.ShapeDtypeStruct(act.shape, bf16),
            jax.ShapeDtypeStruct(weight_two.shape, f32),
            jax.ShapeDtypeStruct(weight_three.shape[::-1], f32),
            *blocks,
        ),
        in_specs=[vmem] * 7,
        out_specs=(vmem,) * 5,
        scratch_shapes=[
            pltpu.VMEM((layers3, chan_three, lanes3), bf16),
            pltpu.VMEM((layers2, lanes2 // local_w, chan_two, local_w), bf16),
            pltpu.VMEM((9, 3 * chan_two, 27 * chan_two), bf16),
            pltpu.VMEM((9, 3 * chan_one, 27 * chan_one), bf16),
            pltpu.VMEM((layers3, 9 * chan_three, inner3), bf16),
            pltpu.VMEM((layers2, 3 * chan_two, lanes2), bf16),
            pltpu.VMEM((3 * chan_two, 9 * chan_three), bf16),
            pltpu.VMEM((9 * chan_one, 3 * chan_two), bf16),
            pltpu.VMEM((layers3 + 2, chan_two, inner3), f32),
            pltpu.VMEM((layers3 - 2, chan_two, 2 * inner3), f32),
            pltpu.VMEM((local_d, 3 * chan_one, lanes2), bf16),
            pltpu.VMEM((local_d // 2 + 2, 3 * chan_two, inner3), bf16),
            pltpu.VMEM((layers2 + 2, chan_one, local_h * local_w), f32),
            pltpu.VMEM(weight_two.shape, f32),
            pltpu.VMEM(weight_three.shape, f32),
            *held,
            pltpu.SemaphoreType.DMA((copies,)),
            pltpu.SemaphoreType.DMA((copies,)),
            pltpu.SemaphoreType.DMA((2,)),
        ],
        compiler_params=pltpu.CompilerParams(
            collective_id=0, has_side_effects=True, vmem_limit_bytes=56 * 2**20
        ),
        name="step",
    )(cot, pre, act, weight_two, weight_three.T, *moments)
    grad_input = grad_input.transpose(2, 0, 1, 3)[None]
    new_weight_three = new_weight_three.T
    mine = lax.axis_index("height")
    new_moment_two, new_moment_three = (
        lax.dynamic_slice_in_dim(block.reshape(-1), mine * moment.shape[0], moment.shape[0])
        for block, moment in ((block_two, moment_two), (block_three, moment_three))
    )
    return (grad_input, new_weight_two, new_weight_three, new_moment_two, new_moment_three)


def solution(mesh):
    in_specs = (
        P("dp", None, "depth", "height", None),
        P("dp", None, "depth", "height", None),
        P("dp", None, "depth", "height"),
        P(),
        P(),
        P(("dp", "depth", "height")),
        P(("dp", "depth", "height")),
    )
    out_specs = (
        P("dp", None, "depth", "height", None),
        P(),
        P(),
        P(("dp", "depth", "height")),
        P(("dp", "depth", "height")),
    )
    return jax.shard_map(local, mesh=mesh, in_specs=in_specs, out_specs=out_specs, check_vma=False)
```
